32 devices in a mesh: seq: 8 (over z, y), head: 4 (over x, core).
Axes of the slice: x: 2, y: 2, z: 4, core: 2. Of those that a mesh axis runs over, the one named last changes fastest.
Arguments:
- queries: bfloat16 [4096, 2048], P('seq', 'head'), may hold values from -6 to 6
- keys: bfloat16 [4096, 2048], P('seq', 'head'), may hold values from -6 to 6
- values: bfloat16 [4096, 2048], P('seq', 'head'), may hold values from -6 to 6
- out_grad: bfloat16 [4096, 4096], P('seq', 'head'), may hold values from -6 to 6
- out_weight: bfloat16 [4096, 2048], P(None, 'head'), may hold values from -0.125 to 0.125
Outputs:
- query_grad: bfloat16 [4096, 2048], P('seq', 'head')
- key_grad: bfloat16 [4096, 2048], P('seq', 'head')
- value_grad: bfloat16 [4096, 2048], P('seq', 'head')
- weight_grad: float32 [4096, 2048], P('seq', 'head')
The draws below stay inside these ranges and needn't reach their ends.
All inputs are finite; a program needn't handle non-finite values.
Results may differ from the reference program's by a relative error of at most 0.0058.
Values may be sent and summed in bfloat16 or wider, within the bound.
No kernel may reach another device: no remote copies, remote signals or barrier semaphores. Data moves between devices by JAX's collectives and lax.ppermute only.
A program may use at most 128 MiB of HBM per device.

```python
import math
import jax
import jax.numpy as jnp
from jax import lax

D = 4096
HEADS = 16
HD = 128
TOK_DEV = 512
TOKENS = 4096
N_SEQ = 8


def spiked(array, rng, source, target, blocks, factor):
    def block_of(position):
        return (jnp.arange(array.shape[position]) // (array.shape[position] // blocks)).reshape((-1,) + (1,) * (array.ndim - 1 - position))

    near = jax.random.permutation(rng, blocks)[block_of(target)]
    far = (block_of(target) + blocks // 2) % blocks
    return jnp.where((block_of(source) == near) | (block_of(source) == far), factor * array, array)


def block_levels(key, extent, pieces, least, top_value):
    def one(axis_at, parts):
        heights = jax.random.uniform(jax.random.fold_in(jax.random.fold_in(key, 6), axis_at), (parts,), jnp.float32, least / len(pieces), top_value / len(pieces))
        return jnp.repeat(jnp.exp(heights), extent[axis_at] // parts).reshape((-1,) + (1,) * (len(extent) - axis_at - 1))

    factor_of = one(*pieces[0])
    for cut in pieces[1:]:
        factor_of = factor_of * one(*cut)
    return factor_of


def scatter_about(own_key, dims, scale, bound, cuts=(), dtype=jnp.bfloat16):
    drawn = jax.random.normal(own_key, dims, jnp.float32) * scale
    if len(cuts) > 0:
        drawn = block_levels(own_key, dims, cuts, -0.22, 0.18) * drawn
    return jnp.clip(drawn, min=-bound, max=bound).astype(dtype)


def gaussian_with(key, dims, width, limit, cuts, heavy, dtype=jnp.bfloat16):
    entries = width * jax.random.normal(key, dims, jnp.float32)
    if cuts:
        entries = entries * block_levels(key, dims, cuts, -0.22, 0.18)
    return jnp.clip(spiked(entries, jax.random.fold_in(key, 3), *heavy), -limit, limit).astype(dtype)


def setup_inputs(seed: int = 0) -> dict:
    seeds = jax.random.split(jax.random.key(seed), 6)
    queries = scatter_about(seeds[0], (TOKENS, HEADS * HD), 1.0, 6.0, ((0, 8), (1, 4)))
    keys = scatter_about(seeds[1], (TOKENS, HEADS * HD), 1.0, 6.0, ((0, 8), (1, 4)))
    values = scatter_about(seeds[2], (TOKENS, HEADS * HD), 1.0, 6.0, ((0, 8), (1, 4)))
    out_grad = gaussian_with(seeds[3], (TOKENS, D), 1.0, 6.0, ((0, 8), (1, 4)), (0, 1, 8, 2.0))
    out_weight = scatter_about(seeds[4], (D, HEADS * HD), (HEADS * HD) ** -0.5, 0.125, ((1, 4),))
    return dict(queries=queries, keys=keys, values=values, out_grad=out_grad, out_weight=out_weight)


def reference(queries, keys, values, out_grad, out_weight):
    scale = 1.0 / math.sqrt(HD * TOKENS)
    attn_grad = jnp.dot(out_grad, out_weight, preferred_element_type=jnp.float32).astype(jnp.bfloat16)
    shape = (N_SEQ, TOK_DEV, HEADS, HD)
    q32 = queries.reshape(shape).astype(jnp.float32)
    k32 = keys.reshape(shape).astype(jnp.float32)
    v32 = values.reshape(shape).astype(jnp.float32)
    d32 = attn_grad.reshape(shape).astype(jnp.float32)
    kv_term = scale * jnp.einsum('ntha,nthb->nhab', k32, v32)
    back_term = scale * jnp.einsum('ntha,nthb->nhab', q32, d32)
    zero = jnp.zeros_like(kv_term[:1])
    prior = jnp.concatenate([zero, jnp.cumsum(kv_term, axis=0)[:-1]], axis=0).astype(jnp.bfloat16)
    later_sum = jnp.flip(jnp.cumsum(jnp.flip(back_term, 0), axis=0), 0)
    later = jnp.concatenate([later_sum[1:], zero], axis=0).astype(jnp.bfloat16)
    mask = jnp.tril(jnp.ones((TOK_DEV, TOK_DEV), jnp.float32))

    def block(index):
        q = q32[index]
        k = k32[index]
        v = v32[index]
        d = d32[index]
        pri = prior[index].astype(jnp.float32)
        lat = later[index].astype(jnp.float32)
        probs = (scale * jnp.einsum('tha,sha->hts', q, k) * mask).astype(jnp.bfloat16).astype(jnp.float32)
        grads = (scale * jnp.einsum('thb,shb->hts', d, v) * mask).astype(jnp.bfloat16).astype(jnp.float32)
        outs = (jnp.einsum('hts,shb->thb', probs, v) + jnp.einsum('tha,hab->thb', q, pri)).astype(jnp.bfloat16)
        dq = (jnp.einsum('hts,sha->tha', grads, k) + jnp.einsum('thb,hab->tha', d, pri)).astype(jnp.bfloat16)
        dk = (jnp.einsum('hts,tha->sha', grads, q) + jnp.einsum('shb,hab->sha', v, lat)).astype(jnp.bfloat16)
        dv = (jnp.einsum('hts,thb->shb', probs, d) + jnp.einsum('sha,hab->shb', k, lat)).astype(jnp.bfloat16)
        return (outs, dq, dk, dv)
    outs, dq, dk, dv = lax.map(block, jnp.arange(N_SEQ))
    flat = (TOKENS, HEADS * HD)
    outs = outs.reshape(flat)
    weight_grad = jnp.dot(out_grad.T, outs, preferred_element_type=jnp.float32) * (1.0 / math.sqrt(TOKENS))
    return (dq.reshape(flat), dk.reshape(flat), dv.reshape(flat), weight_grad)
```

```python
import functools
import math

import jax
import jax.numpy as jnp
from jax import lax
from jax.experimental import pallas as pl
from jax.experimental.pallas import tpu as pltpu
from jax.sharding import PartitionSpec as P

HD = 128
BF16 = jnp.bfloat16
F32 = jnp.float32


def dot(a, b, on_a=1, on_b=0):
    return lax.dot_general(a, b, (((on_a,), (on_b,)), ((), ())), preferred_element_type=F32)


def call(body, outs, *args, scalars=0, vmem=48):
    specs = [pl.BlockSpec(memory_space=pltpu.SMEM)] * scalars
    specs += [pl.BlockSpec(memory_space=pltpu.VMEM)] * (len(args) - scalars)
    return pl.pallas_call(
        body,
        out_shape=outs,
        in_specs=specs,
        out_specs=jax.tree.map(lambda _: pl.BlockSpec(memory_space=pltpu.VMEM), outs),
        compiler_params=pltpu.CompilerParams(vmem_limit_bytes=vmem << 20),
    )(*args)


def head(h):
    return slice(h * HD, (h + 1) * HD)


def state_body(scale, a_ref, b_ref, out_ref):
    for h in range(a_ref.shape[1] // HD):
        term = dot(a_ref[:, head(h)], b_ref[:, head(h)], 0, 0)
        out_ref[head(h), :] = (scale * term).astype(BF16)


def masked(scale, a, b, row):
    scores = scale * dot(a, b, 1, 1)
    rows = row + lax.broadcasted_iota(jnp.int32, scores.shape, 0)
    return jnp.where(lax.broadcasted_iota(jnp.int32, scores.shape, 1) <= rows, scores, 0.0).astype(BF16)


def inner_body(scale, part, q_ref, k_ref, v_ref, out_ref):
    for h in range(q_ref.shape[1] // HD):
        for row in range(0, q_ref.shape[0], part):
            end = row + part
            probs = masked(scale, q_ref[row:end, head(h)], k_ref[:end, head(h)], row)
            out_ref[row:end, head(h)] = dot(probs, v_ref[:end, head(h)])


def outputs_body(first, pv_ref, q_ref, prior_ref, out_ref):
    for i in range(out_ref.shape[1] // HD):
        h = first + i
        total = pv_ref[:, head(h)] + dot(q_ref[:, head(h)], prior_ref[head(h), :])
        out_ref[:, head(i)] = total.astype(BF16)


def attn_grad_body(row_ref, *refs):
    pieces, w_ref, out_ref = refs[:-2], refs[-2], refs[-1]
    total = None
    for i, piece in enumerate(pieces):
        depth = piece.shape[1]
        rows = pl.ds(pl.multiple_of(row_ref[i], depth), depth)
        term = dot(piece[...], w_ref[rows, :])
        total = term if total is None else total + term
    out_ref[...] = total.astype(BF16)


def grads_body(scale, part, q_ref, k_ref, v_ref, d_ref, prior_ref, later_ref, dq_ref, dk_ref, dv_ref):
    rows = q_ref.shape[0]
    for h in range(q_ref.shape[1] // HD):
        at = head(h)
        dk = dot(v_ref[:, at], later_ref[at, :], 1, 1)
        dv = dot(k_ref[:, at], later_ref[at, :])
        dk_parts = [dk[r : r + part] for r in range(0, rows, part)]
        dv_parts = [dv[r : r + part] for r in range(0, rows, part)]
        for row in range(0, rows, part):
            end = row + part
            q, d = q_ref[row:end, at], d_ref[row:end, at]
            probs = masked(scale, q, k_ref[:end, at], row)
            grads = masked(scale, d, v_ref[:end, at], row)
            dq = dot(grads, k_ref[:end, at]) + dot(d, prior_ref[at, :], 1, 1)
            dq_ref[row:end, at] = dq.astype(BF16)
            for i, r in enumerate(range(0, end, part)):
                dk_parts[i] += dot(grads[:, r : r + part], q, 0, 0)
                dv_parts[i] += dot(probs[:, r : r + part], d, 0, 0)
        for i, r in enumerate(range(0, rows, part)):
            dk_ref[r : r + part, at] = dk_parts[i].astype(BF16)
            dv_ref[r : r + part, at] = dv_parts[i].astype(BF16)


def product_body(factor, count, slot_ref, *refs):
    mine, theirs = refs[:count], refs[count : 2 * count]
    o_ref, n_ref = refs[2 * count : 2 * count + 2]
    outs = refs[2 * count + 2 :]
    for s, out in enumerate(outs):
        for j in range(count):

            @pl.when(slot_ref[s] == j)
            def _():
                total = dot(mine[j][...], o_ref[...], 0, 0) + dot(theirs[j][...], n_ref[...], 0, 0)
                out[...] = (factor * total).astype(BF16)


def flip(a, axis, bit, one_way=None):
    pairs = [(i, i ^ bit) for i in range(lax.axis_size(axis))]
    if one_way is not None:
        pairs = [p for p in pairs if bool(p[0] & bit) == one_way]
    return lax.ppermute(a, axis, pairs)


def add(a, b):
    return (a.astype(F32) + b.astype(F32)).astype(BF16)


def scan(term, axis, later):
    size, mine = lax.axis_size(axis), lax.axis_index(axis)
    total, before, bit = term, None, 1
    while bit < size:
        last = 2 * bit == size
        got = flip(total, axis, bit, one_way=later if last else None)
        kept = ((mine & bit) != 0) != later
        take = jnp.where(kept, got, jnp.zeros_like(got))
        before = take if before is None else add(before, take)
        if not last:
            total = add(total, got)
        bit *= 2
    return before


def gather(blocks, axis):
    bit = lax.axis_size(axis)
    blocks = [blocks]
    while bit > 1:
        bit //= 2
        blocks = [item for b in blocks for item in (b, tuple(flip(x, axis, bit) for x in b))]
    return blocks


def line_sum(blocks, line, y, size):
    up = [(0, 1), (3, 2)]
    both = [(0, 1), (1, 0), (2, 3), (3, 2)]
    middle = [(1, 2), (2, 1)]

    def send(a, pairs):
        return lax.ppermute(a, "seq", [(2 * s + i, 2 * t + i) for s, t in pairs for i in range(2)])

    e1 = [send(b[0], up) for b in blocks]
    m2 = [send(add(b[0], r), middle) for b, r in zip(blocks, e1)]
    e2 = [send(b[1], up) for b in blocks]
    m3 = [send(add(b[1], r), middle) for b, r in zip(blocks, e2)]
    e3 = [send(add(b[2], r), both) for b, r in zip(blocks, m2)]
    parts = [
        b[3].astype(F32) + r.astype(F32) + s.astype(F32) for b, r, s in zip(blocks, e3, m3)
    ]
    return jnp.concatenate(parts, axis=1)


ORDER = ((3, 2, 1, 0), (3, 2, 0, 1), (0, 1, 3, 2), (0, 1, 2, 3))


def per_device(queries, keys, values, out_grad, out_weight):
    rows, width = queries.shape
    n_seq, n_head = lax.axis_size("seq"), lax.axis_size("head")
    seq, mine = lax.axis_index("seq"), lax.axis_index("head")
    y, z = seq % 2, seq // 2
    line = n_seq // 2
    total = n_seq * rows
    scale = 1.0 / math.sqrt(HD * total)
    factor = 1.0 / math.sqrt(total)
    part = 256
    shaped = lambda dims, dtype=BF16: jax.ShapeDtypeStruct(dims, dtype)
    state = lambda a, b: call(functools.partial(state_body, scale), shaped((width, HD)), a, b)

    cols = out_grad.shape[1]
    block = cols * n_head // n_seq
    cut = out_grad.reshape(rows, cols // (2 * block), 2, block)
    half = lambda i: lax.dynamic_index_in_dim(cut, i, 2, keepdims=False).reshape(rows, cols // 2)
    own, other = half(y), half(1 - y)

    kv_term = state(keys, values)
    prior = scan(kv_term, "seq", False)
    pv = call(functools.partial(inner_body, scale, part), shaped((rows, width), F32), queries, keys, values)

    pieces = gather((other, own), "head")
    theirs = gather((flip(other, "seq", 1),), "head")

    halves = []
    heads = width // HD
    chunks = 2
    for c in range(chunks):
        o = call(
            functools.partial(outputs_body, c * heads // chunks),
            shaped((rows, width // chunks)),
            pv,
            queries,
            prior,
        )
        halves.append((o, flip(o, "seq", 1)))

    if line == 4 and n_head == 4:
        slots = jnp.asarray(ORDER, jnp.int32)[z] ^ mine
    else:
        slots = jnp.arange(n_head, dtype=jnp.int32) ^ mine
    products = [
        call(
            functools.partial(product_body, factor, n_head),
            [shaped((cols // 2, width // chunks))] * n_head,
            slots,
            *[p[1] for p in pieces],
            *[t[0] for t in theirs],
            o,
            n,
            scalars=1,
        )
        for o, n in halves
    ]
    if line == 4 and n_head == 4:
        weight_grad = line_sum(products, z, y, line)
    else:
        groups = [[2 * p + i for p in range(line)] for i in range(2)]
        whole = jnp.concatenate([jnp.concatenate(p, axis=0) for p in products], axis=1)
        weight_grad = lax.psum_scatter(
            whole.astype(F32), "seq", scatter_dimension=0, axis_index_groups=groups, tiled=True
        )

    flat, starts = [], []
    for j, (n_half, m_half) in enumerate(pieces):
        first = (mine ^ j) * cols
        for i in range(cols // (2 * block)):
            for at, piece in ((1 - y, n_half), (y, m_half)):
                flat.append(piece[:, i * block : (i + 1) * block])
                starts.append(first + (2 * i + at) * block)
    attn_grad = call(
        attn_grad_body,
        shaped((rows, width)),
        jnp.stack(starts).astype(jnp.int32),
        *flat,
        out_weight,
        scalars=1,
    )
    back_term = state(queries, attn_grad)
    later = scan(back_term, "seq", True)
    grads = call(
        functools.partial(grads_body, scale, part),
        [shaped((rows, width))] * 3,
        queries,
        keys,
        values,
        attn_grad,
        prior,
        later,
    )
    return (*grads, weight_grad)


def solution(mesh):
    return jax.shard_map(
        per_device,
        mesh=mesh,
        in_specs=(
            P("seq", "head"),
            P("seq", "head"),
            P("seq", "head"),
            P("seq", "head"),
            P(None, "head"),
        ),
        out_specs=(P("seq", "head"), P("seq", "head"), P("seq", "head"), P("seq", "head")),
        check_vma=False,
    )
```

```python
import functools
import math

import jax
import jax.numpy as jnp
from jax import lax
from jax.experimental import pallas as pl
from jax.experimental.pallas import tpu as pltpu
from jax.sharding import PartitionSpec as P

HD = 128
BF16 = jnp.bfloat16
F32 = jnp.float32


def dot(a, b, on_a=1, on_b=0):
    return lax.dot_general(a, b, (((on_a,), (on_b,)), ((), ())), preferred_element_type=F32)


def call(body, outs, *args, scratch=None, cost=1, vmem=12):
    scratch = [(a.shape, a.dtype) for a in args] if scratch is None else scratch
    count = len(args)

    def kernel(*refs):
        sources, results = refs[:count], refs[count : len(refs) - len(scratch) - 1]
        buffers, sems = refs[len(refs) - len(scratch) - 1 : -1], refs[-1]
        body(sources, results, buffers, sems)

    return pl.pallas_call(
        kernel,
        out_shape=outs,
        in_specs=[pl.BlockSpec(memory_space=pl.ANY)] * count,
        out_specs=jax.tree.map(lambda _: pl.BlockSpec(memory_space=pltpu.VMEM), outs),
        scratch_shapes=[pltpu.VMEM(*buffer) for buffer in scratch]
        + [pltpu.SemaphoreType.DMA((count + len(scratch),))],
        compiler_params=pltpu.CompilerParams(vmem_limit_bytes=vmem << 20),
        cost_estimate=pl.CostEstimate(flops=cost << 20, bytes_accessed=1 << 14, transcendentals=0),
    )(*args)


def fetch(sources, buffers, sems):
    copies = [
        pltpu.make_async_copy(source, buffer, sems.at[i])
        for i, (source, buffer) in enumerate(zip(sources, buffers))
    ]
    for copy in copies:
        copy.start()

    def wait(i):
        copies[i].wait()
        return buffers[i]

    return wait


def head(h):
    return slice(h * HD, (h + 1) * HD)


def state_body(scale, sources, results, buffers, sems):
    split = None
    if len(sources) > 2:
        width = results[1].shape[1]
        first = (1 - lax.rem(lax.axis_index("seq"), 2)) * width
        half = sources[2].at[:, pl.ds(pl.multiple_of(first, width), width)]
        split = pltpu.make_async_copy(half, results[1], sems.at[len(buffers)])
    wait = fetch(sources[:2], buffers, sems)
    if split is not None:
        split.start()
    a_ref, b_ref = wait(0), wait(1)
    for h in range(a_ref.shape[1] // HD):
        term = dot(a_ref[:, head(h)], b_ref[:, head(h)], 0, 0)
        results[0][head(h), :] = (scale * term).astype(BF16)
    if split is not None:
        split.wait()


def masked(scale, a, b, row):
    scores = scale * dot(a, b, 1, 1)
    rows = row + lax.broadcasted_iota(jnp.int32, scores.shape, 0)
    return jnp.where(lax.broadcasted_iota(jnp.int32, scores.shape, 1) <= rows, scores, 0.0).astype(BF16)


def inner_body(scale, part, sources, results, buffers, sems):
    wait = fetch(sources, buffers, sems)
    q_ref, k_ref, v_ref = wait(0), wait(1), wait(2)
    for h in range(q_ref.shape[1] // HD):
        for row in range(0, q_ref.shape[0], part):
            end = row + part
            probs = masked(scale, q_ref[row:end, head(h)], k_ref[:end, head(h)], row)
            results[0][row:end, head(h)] = dot(probs, v_ref[:end, head(h)])


def outputs_body(sources, results, buffers, sems):
    wait = fetch(sources, buffers, sems)
    prior_ref, q_ref, pv_ref = wait(0), wait(1), wait(2)
    for h in range(q_ref.shape[1] // HD):
        total = pv_ref[:, head(h)] + dot(q_ref[:, head(h)], prior_ref[head(h), :])
        results[0][:, head(h)] = total.astype(BF16)


def attn_grad_body(sources, results, buffers, sems):
    wait = fetch(sources, buffers, sems)
    me = lax.axis_index("head")
    w_ref = wait(0)
    total = None
    for j in range(len(sources) - 1):
        piece = wait(j + 1)
        depth = piece.shape[1]
        rows = pl.ds(pl.multiple_of((me ^ j) * depth, depth), depth)
        term = dot(piece[...], w_ref[rows, :])
        total = term if total is None else total + term
    results[0][...] = total.astype(BF16)


def grads_body(scale, part, sources, results, buffers, sems):
    wait = fetch(sources, buffers, sems)
    q_ref, k_ref, v_ref, d_ref, prior_ref, later_ref = (wait(i) for i in range(6))
    dq_ref, dk_ref, dv_ref = results
    rows = q_ref.shape[0]
    for h in range(q_ref.shape[1] // HD):
        at = head(h)
        dk = dot(v_ref[:, at], later_ref[at, :], 1, 1)
        dv = dot(k_ref[:, at], later_ref[at, :])
        dk_parts = [dk[r : r + part] for r in range(0, rows, part)]
        dv_parts = [dv[r : r + part] for r in range(0, rows, part)]
        for row in range(0, rows, part):
            end = row + part
            q, d = q_ref[row:end, at], d_ref[row:end, at]
            probs = masked(scale, q, k_ref[:end, at], row)
            grads = masked(scale, d, v_ref[:end, at], row)
            dq = dot(grads, k_ref[:end, at]) + dot(d, prior_ref[at, :], 1, 1)
            dq_ref[row:end, at] = dq.astype(BF16)
            for i, r in enumerate(range(0, end, part)):
                dk_parts[i] += dot(grads[:, r : r + part], q, 0, 0)
                dv_parts[i] += dot(probs[:, r : r + part], d, 0, 0)
        for i, r in enumerate(range(0, rows, part)):
            dk_ref[r : r + part, at] = dk_parts[i].astype(BF16)
            dv_ref[r : r + part, at] = dv_parts[i].astype(BF16)


def slot(z, i):
    at = jnp.int32(ORDER[-1][i])
    for p in range(len(ORDER) - 1):
        at = jnp.where(z == p, ORDER[p][i], at)
    return at


def product_body(factor, count, short, slots, sources, results, buffers, sems):
    used = len(slots)
    seq, me = lax.axis_index("seq"), lax.axis_index("head")
    o, n = (pltpu.make_async_copy(sources[i], buffers[i], sems.at[i]) for i in range(2))
    o.start()
    n.start()
    copies = []
    for i, s in enumerate(slots):
        which = (slot(lax.div(seq, 2), s) if short else s) ^ me
        for part in range(2):
            at = 2 + part * used + i
            for j in range(count):

                @pl.when(which == j)
                def _():
                    piece = sources[2 + part * count + j]
                    width = buffers[at].shape[1]
                    if piece.shape[1] != width:
                        first = pl.multiple_of(lax.rem(seq, 2) * width, width)
                        piece = piece.at[:, pl.ds(first, width)]
                    pltpu.make_async_copy(piece, buffers[at], sems.at[at]).start()

            copies.append(pltpu.make_async_copy(buffers[at], buffers[at], sems.at[at]))
    o.wait()
    n.wait()
    for i, out in enumerate(results):
        copies[2 * i].wait()
        copies[2 * i + 1].wait()
        total = dot(buffers[2 + i][...], buffers[0][...], 0, 0)
        total += dot(buffers[2 + used + i][...], buffers[1][...], 0, 0)
        out[...] = (factor * total).astype(out.dtype)


def phase(*values):
    return lax.optimization_barrier(values)


def flip(a, axis, bit):
    return lax.ppermute(a, axis, [(i, i ^ bit) for i in range(lax.axis_size(axis))])


def add(a, b):
    return (a.astype(F32) + b.astype(F32)).astype(BF16)


class Scan:
    def __init__(self, term, later):
        self.term, self.later, self.total, self.before = term, later, term, 0.0
        self.bits = [1 << i for i in range(lax.axis_size("seq").bit_length() - 1)]

    def inside(self, bit):
        return ((lax.axis_index("seq") & bit) != 0) != self.later

    def start(self, bit):
        return flip(self.total, "seq", bit)

    def take(self, bit, got):
        self.before += jnp.where(self.inside(bit), got, 0).astype(F32)
        self.total = add(self.total, got)

    def across(self):
        own = jnp.where(self.inside(1), 0, self.term).astype(F32)
        return flip((self.before + own).astype(BF16), "seq", 1)

    def result(self, got=0.0):
        return (self.before + got).astype(BF16)


def send(a, pairs):
    return lax.ppermute(a, "seq", [(2 * s + i, 2 * t + i) for s, t in pairs for i in range(2)])


OUTER = ((0, 1), (1, 0), (2, 3), (3, 2))
MIDDLE = ((1, 2), (2, 1))
ORDER = ((3, 2, 1, 0), (3, 2, 0, 1), (0, 1, 3, 2), (0, 1, 2, 3))


def per_device(queries, keys, values, out_grad, out_weight):
    rows, width = queries.shape
    n_seq, n_head = lax.axis_size("seq"), lax.axis_size("head")
    seq = lax.axis_index("seq")
    y = seq % 2
    line = n_seq // 2
    total = n_seq * rows
    scale = 1.0 / math.sqrt(HD * total)
    factor = 1.0 / math.sqrt(total)
    part = 256
    shaped = lambda dims, dtype=BF16: jax.ShapeDtypeStruct(dims, dtype)
    state = functools.partial(state_body, scale)
    state_shape = shaped((width, HD))

    cols = out_grad.shape[1]
    block = cols * n_head // n_seq
    short = line == 4 and n_head == 4

    def half(a, i):
        cut = a.reshape(rows, cols // (2 * block), 2, block)
        return lax.dynamic_index_in_dim(cut, i, 2, keepdims=False).reshape(rows, cols // 2)

    inner = functools.partial(inner_body, scale, part)
    outputs = outputs_body
    matrix = shaped((rows, width))

    def product(slots, kinds, *operands, cost=1):
        body = functools.partial(product_body, factor, n_head, short, slots)
        outs = [shaped((cols // 2, width), kind) for kind in kinds]
        like = [((rows, cols // 2), BF16)] * (2 * len(slots))
        scratch = [((rows, width), BF16)] * 2 + like
        return call(body, outs, *operands, scratch=scratch, cost=cost, vmem=60)

    by_x = flip(out_grad, "head", 2)
    if short:
        scratch = [((rows, width), BF16)] * 2
        outs = [state_shape, shaped((rows, cols // 2))]
        kv_term, other = call(state, outs, keys, values, out_grad, scratch=scratch)
    else:
        (kv_term,), other = call(state, [state_shape], keys, values), half(out_grad, 1 - y)
    prior = Scan(kv_term, False)
    got = prior.start(1)
    near = flip(other, "seq", 1)
    got, q, grad = phase(got, queries, out_grad)
    prior.take(1, got)
    for bit in prior.bits[1:]:
        got = prior.start(bit)
        if bit == 4:
            (pv,) = call(inner, [shaped((rows, width), F32)], q, keys, values)
            got, pv, grad, by_x, near = phase(got, pv, grad, by_x, near)
        prior.take(bit, got)
    prior = prior.result()

    (o,) = call(outputs, [matrix], prior, queries, pv)
    o, by_x, near, grad = phase(o, by_x, near, grad)
    n = flip(o, "seq", 1)
    far = flip(near, "head", 2)
    by_core, by_xc, near_c = (flip(a, "head", 1) for a in (grad, by_x, near))

    pieces = [out_grad, by_core, by_x, by_xc]
    mine = pieces if short else [half(p, y) for p in pieces]
    (attn_grad,) = call(attn_grad_body, [matrix], out_weight, *pieces)
    (back_term,) = call(state, [state_shape], queries, attn_grad)
    later = Scan(back_term, True)
    got = later.start(2)
    got, n, far = phase(got, n, far)
    far_c = flip(far, "head", 1)
    later.take(2, got)
    operands = (o, n, *mine, near, near_c, far, far_c)

    def gradients(later):
        body = functools.partial(grads_body, scale, part)
        return call(body, [matrix] * 3, queries, keys, values, attn_grad, prior, later)

    if short:
        got = later.start(4)
        (b0,) = product((0,), (BF16,), *operands)
        e1 = send(b0, OUTER)
        o, got, _ = phase(o, got, b0)
        b1, b2, b3 = product((1, 2, 3), (BF16, F32, F32), o, *operands[1:], cost=1 << 14)
        later.take(4, got)
        got = later.across()
        e2 = send(b1, OUTER)
        e1, got, b2 = phase(e1, got, b2)
        m2 = send(add(b0, e1), MIDDLE)
        grads = gradients(later.result(got))
        e2, *grads = phase(e2, *grads)
        m3 = send(add(b1, e2), MIDDLE)
        e3 = send(add(b2, m2), OUTER)
        weight_grad = b3 + e3.astype(F32) + m3.astype(F32)
    else:
        for bit in later.bits[1:]:
            later.take(bit, later.start(bit))
        grads = gradients(later.result(later.across()))
        groups = [[2 * p + i for p in range(line)] for i in range(2)]
        whole = jnp.concatenate(product(range(n_head), [F32] * n_head, *operands), axis=0)
        weight_grad = lax.psum_scatter(
            whole, "seq", scatter_dimension=0, axis_index_groups=groups, tiled=True
        )
    return (*grads, weight_grad)


def solution(mesh):
    return jax.shard_map(
        per_device,
        mesh=mesh,
        in_specs=(
            P("seq", "head"),
            P("seq", "head"),
            P("seq", "head"),
            P("seq", "head"),
            P(None, "head"),
        ),
        out_specs=(P("seq", "head"), P("seq", "head"), P("seq", "head"), P("seq", "head")),
        check_vma=False,
    )
```

```python
import functools
import math

import jax
import jax.numpy as jnp
from jax import lax
from jax.experimental import pallas as pl
from jax.experimental.pallas import tpu as pltpu
from jax.sharding import PartitionSpec as P

HD = 128
BF16 = jnp.bfloat16
F32 = jnp.float32


def dot(a, b, on_a=1, on_b=0):
    return lax.dot_general(a, b, (((on_a,), (on_b,)), ((), ())), preferred_element_type=F32)


def call(body, outs, *args, scratch=None, cost=1, vmem=12):
    scratch = [(a.shape, a.dtype) for a in args] if scratch is None else scratch
    count = len(args)

    def kernel(*refs):
        sources, results = refs[:count], refs[count : len(refs) - len(scratch) - 1]
        buffers, sems = refs[len(refs) - len(scratch) - 1 : -1], refs[-1]
        body(sources, results, buffers, sems)

    return pl.pallas_call(
        kernel,
        out_shape=outs,
        in_specs=[pl.BlockSpec(memory_space=pl.ANY)] * count,
        out_specs=jax.tree.map(lambda _: pl.BlockSpec(memory_space=pltpu.VMEM), outs),
        scratch_shapes=[pltpu.VMEM(*buffer) for buffer in scratch]
        + [pltpu.SemaphoreType.DMA((count + len(scratch),))],
        compiler_params=pltpu.CompilerParams(vmem_limit_bytes=vmem << 20),
        cost_estimate=pl.CostEstimate(flops=cost << 20, bytes_accessed=1 << 14, transcendentals=0),
    )(*args)


def fetch(sources, buffers, sems):
    copies = [
        pltpu.make_async_copy(source, buffer, sems.at[i])
        for i, (source, buffer) in enumerate(zip(sources, buffers))
    ]
    for copy in copies:
        copy.start()

    def wait(i):
        copies[i].wait()
        return buffers[i]

    return wait


def head(h):
    return slice(h * HD, (h + 1) * HD)


def state_body(scale, sources, results, buffers, sems):
    split = None
    if len(sources) > 2:
        width = results[1].shape[1]
        first = (1 - lax.rem(lax.axis_index("seq"), 2)) * width
        half = sources[2].at[:, pl.ds(pl.multiple_of(first, width), width)]
        split = pltpu.make_async_copy(half, results[1], sems.at[len(buffers)])
    wait = fetch(sources[:2], buffers, sems)
    if split is not None:
        split.start()
    a_ref, b_ref = wait(0), wait(1)
    for h in range(a_ref.shape[1] // HD):
        term = dot(a_ref[:, head(h)], b_ref[:, head(h)], 0, 0)
        results[0][head(h), :] = (scale * term).astype(BF16)
    if split is not None:
        split.wait()


def masked(scale, a, b, row):
    scores = scale * dot(a, b, 1, 1)
    rows = row + lax.broadcasted_iota(jnp.int32, scores.shape, 0)
    return jnp.where(lax.broadcasted_iota(jnp.int32, scores.shape, 1) <= rows, scores, 0.0).astype(BF16)


def inner_body(scale, part, sources, results, buffers, sems):
    wait = fetch(sources, buffers, sems)
    q_ref, k_ref, v_ref = wait(0), wait(1), wait(2)
    for h in range(q_ref.shape[1] // HD):
        for row in range(0, q_ref.shape[0], part):
            end = row + part
            probs = masked(scale, q_ref[row:end, head(h)], k_ref[:end, head(h)], row)
            results[0][row:end, head(h)] = dot(probs, v_ref[:end, head(h)])


def outputs_body(sources, results, buffers, sems):
    wait = fetch(sources, buffers, sems)
    prior_ref, q_ref, pv_ref = wait(0), wait(1), wait(2)
    for h in range(q_ref.shape[1] // HD):
        total = pv_ref[:, head(h)] + dot(q_ref[:, head(h)], prior_ref[head(h), :])
        results[0][:, head(h)] = total.astype(BF16)


def attn_grad_body(sources, results, buffers, sems):
    wait = fetch(sources, buffers, sems)
    me = lax.axis_index("head")
    w_ref = wait(0)
    total = None
    for j in range(len(sources) - 1):
        piece = wait(j + 1)
        depth = piece.shape[1]
        rows = pl.ds(pl.multiple_of((me ^ j) * depth, depth), depth)
        term = dot(piece[...], w_ref[rows, :])
        total = term if total is None else total + term
    results[0][...] = total.astype(BF16)


def grads_body(scale, part, sources, results, buffers, sems):
    wait = fetch(sources, buffers, sems)
    q_ref, k_ref, v_ref, d_ref, prior_ref, later_ref = (wait(i) for i in range(6))
    dq_ref, dk_ref, dv_ref = results
    rows = q_ref.shape[0]
    for h in range(q_ref.shape[1] // HD):
        at = head(h)
        dk = dot(v_ref[:, at], later_ref[at, :], 1, 1)
        dv = dot(k_ref[:, at], later_ref[at, :])
        dk_parts = [dk[r : r + part] for r in range(0, rows, part)]
        dv_parts = [dv[r : r + part] for r in range(0, rows, part)]
        for row in range(0, rows, part):
            end = row + part
            q, d = q_ref[row:end, at], d_ref[row:end, at]
            probs = masked(scale, q, k_ref[:end, at], row)
            grads = masked(scale, d, v_ref[:end, at], row)
            dq = dot(grads, k_ref[:end, at]) + dot(d, prior_ref[at, :], 1, 1)
            dq_ref[row:end, at] = dq.astype(BF16)
            for i, r in enumerate(range(0, end, part)):
                dk_parts[i] += dot(grads[:, r : r + part], q, 0, 0)
                dv_parts[i] += dot(probs[:, r : r + part], d, 0, 0)
        for i, r in enumerate(range(0, rows, part)):
            dk_ref[r : r + part, at] = dk_parts[i].astype(BF16)
            dv_ref[r : r + part, at] = dv_parts[i].astype(BF16)


def slot(z, i):
    at = jnp.int32(ORDER[-1][i])
    for p in range(len(ORDER) - 1):
        at = jnp.where(z == p, ORDER[p][i], at)
    return at


def product_body(factor, count, short, slots, parts, sources, results, buffers, sems):
    used = len(slots)
    seq, me = lax.axis_index("seq"), lax.axis_index("head")
    o, n = (pltpu.make_async_copy(sources[i], buffers[i], sems.at[i]) for i in range(2))
    o.start()
    n.start()
    copies = []
    for i, s in enumerate(slots):
        which = (slot(lax.div(seq, 2), s) if short else s) ^ me
        for part in range(2):
            at = 2 + part * used + i
            for j in range(count):

                @pl.when(which == j)
                def _():
                    piece = sources[2 + part * count + j]
                    width = buffers[at].shape[1]
                    if piece.shape[1] != width:
                        first = pl.multiple_of(lax.rem(seq, 2) * width, width)
                        piece = piece.at[:, pl.ds(first, width)]
                    pltpu.make_async_copy(piece, buffers[at], sems.at[at]).start()

            copies.append(pltpu.make_async_copy(buffers[at], buffers[at], sems.at[at]))
    o.wait()
    n.wait()
    results = list(results)
    for i in range(used):
        copies[2 * i].wait()
        copies[2 * i + 1].wait()
        total = dot(buffers[2 + i][...], buffers[0][...], 0, 0)
        total += dot(buffers[2 + used + i][...], buffers[1][...], 0, 0)
        total *= factor
        first = 0
        for _ in range(parts[i]):
            part = results.pop(0)
            part[...] = total[:, first : first + part.shape[1]].astype(part.dtype)
            first += part.shape[1]


def phase(*values):
    return lax.optimization_barrier(values)


def flip(a, axis, bit):
    return lax.ppermute(a, axis, [(i, i ^ bit) for i in range(lax.axis_size(axis))])


def add_body(*refs):
    *sources, out = refs
    out[...] = sum(ref[...].astype(F32) for ref in sources).astype(out.dtype)


def add(*terms, kind=BF16):
    spec = pl.BlockSpec(memory_space=pltpu.VMEM)
    return pl.pallas_call(
        add_body,
        out_shape=jax.ShapeDtypeStruct(terms[0].shape, kind),
        in_specs=[spec] * len(terms),
        out_specs=spec,
        compiler_params=pltpu.CompilerParams(vmem_limit_bytes=8 << 20),
        cost_estimate=pl.CostEstimate(flops=1 << 20, bytes_accessed=1 << 14, transcendentals=0),
    )(*terms)


class Scan:
    def __init__(self, term, later):
        self.term, self.later, self.total, self.before = term, later, term, 0.0
        self.bits = [1 << i for i in range(lax.axis_size("seq").bit_length() - 1)]

    def inside(self, bit):
        return ((lax.axis_index("seq") & bit) != 0) != self.later

    def start(self, bit):
        return flip(self.total, "seq", bit)

    def take(self, bit, got):
        self.before += jnp.where(self.inside(bit), got, 0).astype(F32)
        self.total = add(self.total, got)

    def across(self):
        own = jnp.where(self.inside(1), 0, self.term).astype(F32)
        return flip((self.before + own).astype(BF16), "seq", 1)

    def result(self, got=0.0):
        return (self.before + got).astype(BF16)


def send(a, pairs):
    return lax.ppermute(a, "seq", [(2 * s + i, 2 * t + i) for s, t in pairs for i in range(2)])


OUTER = ((0, 1), (1, 0), (2, 3), (3, 2))
MIDDLE = ((1, 2), (2, 1))
ORDER = ((3, 2, 1, 0), (3, 2, 0, 1), (0, 1, 3, 2), (0, 1, 2, 3))


def per_device(queries, keys, values, out_grad, out_weight):
    rows, width = queries.shape
    n_seq, n_head = lax.axis_size("seq"), lax.axis_size("head")
    seq = lax.axis_index("seq")
    y = seq % 2
    line = n_seq // 2
    total = n_seq * rows
    scale = 1.0 / math.sqrt(HD * total)
    factor = 1.0 / math.sqrt(total)
    part = 256
    shaped = lambda dims, dtype=BF16: jax.ShapeDtypeStruct(dims, dtype)
    state = functools.partial(state_body, scale)
    state_shape = shaped((width, HD))

    cols = out_grad.shape[1]
    block = cols * n_head // n_seq
    short = line == 4 and n_head == 4

    def half(a, i):
        cut = a.reshape(rows, cols // (2 * block), 2, block)
        return lax.dynamic_index_in_dim(cut, i, 2, keepdims=False).reshape(rows, cols // 2)

    inner = functools.partial(inner_body, scale, part)
    outputs = outputs_body
    matrix = shaped((rows, width))

    def product(slots, kinds, *operands, cost=1):
        body = functools.partial(product_body, factor, n_head, short, slots, [len(k) for k in kinds])
        outs = [shaped((cols // 2, width // len(k)), kind) for k in kinds for kind in k]
        like = [((rows, cols // 2), BF16)] * (2 * len(slots))
        scratch = [((rows, width), BF16)] * 2 + like
        return call(body, outs, *operands, scratch=scratch, cost=cost, vmem=60)

    by_x = flip(out_grad, "head", 2)
    if short:
        scratch = [((rows, width), BF16)] * 2
        outs = [state_shape, shaped((rows, cols // 2))]
        kv_term, other = call(state, outs, keys, values, out_grad, scratch=scratch, vmem=60)
    else:
        (kv_term,), other = call(state, [state_shape], keys, values), half(out_grad, 1 - y)
    prior = Scan(kv_term, False)
    got = prior.start(1)
    got, other, q, grad = phase(got, other, queries, out_grad)
    near = flip(other, "seq", 1)
    prior.take(1, got)
    for bit in prior.bits[1:]:
        got = prior.start(bit)
        if bit == 4:
            (pv,) = call(inner, [shaped((rows, width), F32)], q, keys, values)
            got, pv, grad, by_x, near = phase(got, pv, grad, by_x, near)
        prior.take(bit, got)
    prior = prior.result()

    (o,) = call(outputs, [matrix], prior, queries, pv)
    o, by_x, near, grad = phase(o, by_x, near, grad)
    n = flip(o, "seq", 1)
    far = flip(near, "head", 2)
    by_core, by_xc, near_c = (flip(a, "head", 1) for a in (grad, by_x, near))

    pieces = [out_grad, by_core, by_x, by_xc]
    mine = pieces if short else [half(p, y) for p in pieces]
    (attn_grad,) = call(attn_grad_body, [matrix], out_weight, *pieces)
    (back_term,) = call(state, [state_shape], queries, attn_grad)
    later = Scan(back_term, True)
    got = later.start(2)
    got, n, far = phase(got, n, far)
    far_c = flip(far, "head", 1)
    later.take(2, got)
    operands = (o, n, *mine, near, near_c, far, far_c)

    def gradients(later):
        body = functools.partial(grads_body, scale, part)
        return call(body, [matrix] * 3, queries, keys, values, attn_grad, prior, later)

    if short:
        got = later.start(4)
        *b0, b1 = product((0, 1), ((BF16,) * 2, (BF16,)), *operands)
        e1, e2 = [send(b, OUTER) for b in b0], send(b1, OUTER)
        o, got, *b0 = phase(o, got, *b0)
        b2, b3 = product((2, 3), ((F32,), (F32,)), o, *operands[1:], cost=1 << 14)
        later.take(4, got)
        got = later.across()
        e1[0], got, b2 = phase(e1[0], got, b2)
        m2 = [send(add(b, e), MIDDLE) for b, e in zip(b0, e1)]
        e2, got, *m2 = phase(e2, got, *m2)
        grads = gradients(later.result(got))
        m3 = send(add(b1, e2), MIDDLE)
        e3 = send(add(b2, jnp.concatenate(m2, axis=1)), OUTER)
        weight_grad = add(b3, e3, m3, kind=F32)
    else:
        for bit in later.bits[1:]:
            later.take(bit, later.start(bit))
        grads = gradients(later.result(later.across()))
        groups = [[2 * p + i for p in range(line)] for i in range(2)]
        whole = jnp.concatenate(product(range(n_head), [(F32,)] * n_head, *operands), axis=0)
        weight_grad = lax.psum_scatter(
            whole, "seq", scatter_dimension=0, axis_index_groups=groups, tiled=True
        )
    return (*grads, weight_grad)


def solution(mesh):
    return jax.shard_map(
        per_device,
        mesh=mesh,
        in_specs=(
            P("seq", "head"),
            P("seq", "head"),
            P("seq", "head"),
            P("seq", "head"),
            P(None, "head"),
        ),
        out_specs=(P("seq", "head"), P("seq", "head"), P("seq", "head"), P("seq", "head")),
        check_vma=False,
    )
```

```python
import functools
import math

import jax
import jax.numpy as jnp
from jax import lax
from jax.experimental import pallas as pl
from jax.experimental.pallas import tpu as pltpu
from jax.sharding import PartitionSpec as P

HD = 128
BF16 = jnp.bfloat16
F32 = jnp.float32


def dot(a, b, on_a=1, on_b=0):
    return lax.dot_general(a, b, (((on_a,), (on_b,)), ((), ())), preferred_element_type=F32)


def call(body, outs, *args, scratch=None, cost=1, vmem=12):
    scratch = [(a.shape, a.dtype) for a in args] if scratch is None else scratch
    count = len(args)

    def kernel(*refs):
        sources, results = refs[:count], refs[count : len(refs) - len(scratch) - 1]
        buffers, sems = refs[len(refs) - len(scratch) - 1 : -1], refs[-1]
        body(sources, results, buffers, sems)

    return pl.pallas_call(
        kernel,
        out_shape=outs,
        in_specs=[pl.BlockSpec(memory_space=pl.ANY)] * count,
        out_specs=jax.tree.map(lambda _: pl.BlockSpec(memory_space=pltpu.VMEM), outs),
        scratch_shapes=[pltpu.VMEM(*buffer) for buffer in scratch]
        + [pltpu.SemaphoreType.DMA((count + len(scratch),))],
        compiler_params=pltpu.CompilerParams(vmem_limit_bytes=vmem << 20),
        cost_estimate=pl.CostEstimate(flops=cost << 20, bytes_accessed=1 << 14, transcendentals=0),
    )(*args)


def fetch(sources, buffers, sems):
    copies = [
        pltpu.make_async_copy(source, buffer, sems.at[i])
        for i, (source, buffer) in enumerate(zip(sources, buffers))
    ]
    for copy in copies:
        copy.start()

    def wait(i):
        copies[i].wait()
        return buffers[i]

    return wait


def head(h):
    return slice(h * HD, (h + 1) * HD)


def state_body(scale, sources, results, buffers, sems):
    split = None
    if len(sources) > 2:
        width = results[1].shape[1]
        first = (1 - lax.rem(lax.axis_index("seq"), 2)) * width
        half = sources[2].at[:, pl.ds(pl.multiple_of(first, width), width)]
        split = pltpu.make_async_copy(half, results[1], sems.at[len(buffers)])
    wait = fetch(sources[:2], buffers, sems)
    if split is not None:
        split.start()
    a_ref, b_ref = wait(0), wait(1)
    for h in range(a_ref.shape[1] // HD):
        term = dot(a_ref[:, head(h)], b_ref[:, head(h)], 0, 0)
        results[0][head(h), :] = (scale * term).astype(BF16)
    if split is not None:
        split.wait()


def masked(scale, a, b, row):
    scores = scale * dot(a, b, 1, 1)
    rows = row + lax.broadcasted_iota(jnp.int32, scores.shape, 0)
    return jnp.where(lax.broadcasted_iota(jnp.int32, scores.shape, 1) <= rows, scores, 0.0).astype(BF16)


def inner_body(scale, part, sources, results, buffers, sems):
    wait = fetch(sources, buffers, sems)
    q_ref, k_ref, v_ref = wait(0), wait(1), wait(2)
    for h in range(q_ref.shape[1] // HD):
        for row in range(0, q_ref.shape[0], part):
            end = row + part
            probs = masked(scale, q_ref[row:end, head(h)], k_ref[:end, head(h)], row)
            results[0][row:end, head(h)] = dot(probs, v_ref[:end, head(h)])


def outputs_body(sources, results, buffers, sems):
    wait = fetch(sources, buffers, sems)
    prior_ref, q_ref, pv_ref = wait(0), wait(1), wait(2)
    for h in range(q_ref.shape[1] // HD):
        total = pv_ref[:, head(h)] + dot(q_ref[:, head(h)], prior_ref[head(h), :])
        results[0][:, head(h)] = total.astype(BF16)


def attn_grad_body(sources, results, buffers, sems):
    wait = fetch(sources, buffers, sems)
    me = lax.axis_index("head")
    w_ref = wait(0)
    total = None
    for j in range(len(sources) - 1):
        piece = wait(j + 1)
        depth = piece.shape[1]
        rows = pl.ds(pl.multiple_of((me ^ j) * depth, depth), depth)
        term = dot(piece[...], w_ref[rows, :])
        total = term if total is None else total + term
    results[0][...] = total.astype(BF16)


def grads_body(scale, part, sources, results, buffers, sems):
    wait = fetch(sources, buffers, sems)
    q_ref, k_ref, v_ref, d_ref, prior_ref, later_ref = (wait(i) for i in range(6))
    dq_ref, dk_ref, dv_ref = results
    rows = q_ref.shape[0]
    for h in range(q_ref.shape[1] // HD):
        at = head(h)
        dk = dot(v_ref[:, at], later_ref[at, :], 1, 1)
        dv = dot(k_ref[:, at], later_ref[at, :])
        dk_parts = [dk[r : r + part] for r in range(0, rows, part)]
        dv_parts = [dv[r : r + part] for r in range(0, rows, part)]
        for row in range(0, rows, part):
            end = row + part
            q, d = q_ref[row:end, at], d_ref[row:end, at]
            probs = masked(scale, q, k_ref[:end, at], row)
            grads = masked(scale, d, v_ref[:end, at], row)
            dq = dot(grads, k_ref[:end, at]) + dot(d, prior_ref[at, :], 1, 1)
            dq_ref[row:end, at] = dq.astype(BF16)
            for i, r in enumerate(range(0, end, part)):
                dk_parts[i] += dot(grads[:, r : r + part], q, 0, 0)
                dv_parts[i] += dot(probs[:, r : r + part], d, 0, 0)
        for i, r in enumerate(range(0, rows, part)):
            dk_ref[r : r + part, at] = dk_parts[i].astype(BF16)
            dv_ref[r : r + part, at] = dv_parts[i].astype(BF16)


def slot(z, i):
    at = jnp.int32(ORDER[-1][i])
    for p in range(len(ORDER) - 1):
        at = jnp.where(z == p, ORDER[p][i], at)
    return at


def product_body(factor, count, short, slots, parts, sources, results, buffers, sems):
    used = len(slots)
    seq, me = lax.axis_index("seq"), lax.axis_index("head")
    o, n = (pltpu.make_async_copy(sources[i], buffers[i], sems.at[i]) for i in range(2))
    o.start()
    n.start()
    copies = []
    for i, s in enumerate(slots):
        which = (slot(lax.div(seq, 2), s) if short else s) ^ me
        for part in range(2):
            at = 2 + part * used + i
            for j in range(count):

                @pl.when(which == j)
                def _():
                    piece = sources[2 + part * count + j]
                    width = buffers[at].shape[1]
                    if piece.shape[1] != width:
                        first = pl.multiple_of(lax.rem(seq, 2) * width, width)
                        piece = piece.at[:, pl.ds(first, width)]
                    pltpu.make_async_copy(piece, buffers[at], sems.at[at]).start()

            copies.append(pltpu.make_async_copy(buffers[at], buffers[at], sems.at[at]))
    o.wait()
    n.wait()
    results = list(results)
    for i in range(used):
        copies[2 * i].wait()
        copies[2 * i + 1].wait()
        total = dot(buffers[2 + i][...], buffers[0][...], 0, 0)
        total += dot(buffers[2 + used + i][...], buffers[1][...], 0, 0)
        total *= factor
        first = 0
        for _ in range(parts[i]):
            part = results.pop(0)
            part[...] = total[:, first : first + part.shape[1]].astype(part.dtype)
            first += part.shape[1]


def phase(*values):
    return lax.optimization_barrier(values)


def flip(a, axis, bit):
    return lax.ppermute(a, axis, [(i, i ^ bit) for i in range(lax.axis_size(axis))])


def add_body(*refs):
    *sources, out = refs
    out[...] = sum(ref[...].astype(F32) for ref in sources).astype(out.dtype)


def add(*terms, kind=BF16, cost=1):
    spec = pl.BlockSpec(memory_space=pltpu.VMEM)
    return pl.pallas_call(
        add_body,
        out_shape=jax.ShapeDtypeStruct(terms[0].shape, kind),
        in_specs=[spec] * len(terms),
        out_specs=spec,
        compiler_params=pltpu.CompilerParams(vmem_limit_bytes=8 << 20),
        cost_estimate=pl.CostEstimate(flops=cost << 20, bytes_accessed=1 << 14, transcendentals=0),
    )(*terms)


def total_body(b_ref, e_ref, *refs):
    *m_refs, out_ref = refs
    width = out_ref.shape[1] // len(m_refs)
    for i, m_ref in enumerate(m_refs):
        at = slice(i * width, (i + 1) * width)
        out_ref[:, at] = b_ref[:, at] + e_ref[:, at].astype(F32) + m_ref[...].astype(F32)


def joined_body(b_ref, *refs):
    *m_refs, out_ref = refs
    width = out_ref.shape[1] // len(m_refs)
    for i, m_ref in enumerate(m_refs):
        at = slice(i * width, (i + 1) * width)
        out_ref[:, at] = (b_ref[:, at] + m_ref[...].astype(F32)).astype(BF16)


def small(body, kind, *terms):
    spec = pl.BlockSpec(memory_space=pltpu.VMEM)
    return pl.pallas_call(
        body,
        out_shape=jax.ShapeDtypeStruct(terms[0].shape, kind),
        in_specs=[spec] * len(terms),
        out_specs=spec,
        compiler_params=pltpu.CompilerParams(vmem_limit_bytes=8 << 20),
        cost_estimate=pl.CostEstimate(flops=1 << 20, bytes_accessed=1 << 14, transcendentals=0),
    )(*terms)


class Scan:
    def __init__(self, term, later):
        self.term, self.later, self.total, self.before = term, later, term, 0.0
        self.bits = [1 << i for i in range(lax.axis_size("seq").bit_length() - 1)]

    def inside(self, bit):
        return ((lax.axis_index("seq") & bit) != 0) != self.later

    def start(self, bit):
        return flip(self.total, "seq", bit)

    def take(self, bit, got):
        self.before += jnp.where(self.inside(bit), got, 0).astype(F32)
        self.total = add(self.total, got)

    def across(self):
        own = jnp.where(self.inside(1), 0, self.term).astype(F32)
        return flip((self.before + own).astype(BF16), "seq", 1)

    def result(self, got=0.0):
        return (self.before + got).astype(BF16)


def send(a, pairs):
    return lax.ppermute(a, "seq", [(2 * s + i, 2 * t + i) for s, t in pairs for i in range(2)])


OUTER = ((0, 1), (1, 0), (2, 3), (3, 2))
MIDDLE = ((1, 2), (2, 1))
ORDER = ((3, 2, 1, 0), (3, 2, 0, 1), (0, 1, 3, 2), (0, 1, 2, 3))


def per_device(queries, keys, values, out_grad, out_weight):
    rows, width = queries.shape
    n_seq, n_head = lax.axis_size("seq"), lax.axis_size("head")
    seq = lax.axis_index("seq")
    y = seq % 2
    line = n_seq // 2
    total = n_seq * rows
    scale = 1.0 / math.sqrt(HD * total)
    factor = 1.0 / math.sqrt(total)
    part = 256
    shaped = lambda dims, dtype=BF16: jax.ShapeDtypeStruct(dims, dtype)
    state = functools.partial(state_body, scale)
    state_shape = shaped((width, HD))

    cols = out_grad.shape[1]
    block = cols * n_head // n_seq
    short = line == 4 and n_head == 4

    def half(a, i):
        cut = a.reshape(rows, cols // (2 * block), 2, block)
        return lax.dynamic_index_in_dim(cut, i, 2, keepdims=False).reshape(rows, cols // 2)

    inner = functools.partial(inner_body, scale, part)
    outputs = outputs_body
    matrix = shaped((rows, width))

    def product(slots, kinds, *operands, cost=1):
        body = functools.partial(product_body, factor, n_head, short, slots, [len(k) for k in kinds])
        outs = [shaped((cols // 2, width // len(k)), kind) for k in kinds for kind in k]
        like = [((rows, cols // 2), BF16)] * (2 * len(slots))
        scratch = [((rows, width), BF16)] * 2 + like
        return call(body, outs, *operands, scratch=scratch, cost=cost, vmem=60)

    by_x = flip(out_grad, "head", 2)
    if short:
        scratch = [((rows, width), BF16)] * 2
        outs = [state_shape, shaped((rows, cols // 2))]
        kv_term, other = call(state, outs, keys, values, out_grad, scratch=scratch, vmem=60)
    else:
        (kv_term,), other = call(state, [state_shape], keys, values), half(out_grad, 1 - y)
    prior = Scan(kv_term, False)
    got = prior.start(1)
    got, other, q, grad = phase(got, other, queries, out_grad)
    near = flip(other, "seq", 1)
    prior.take(1, got)
    for bit in prior.bits[1:]:
        got = prior.start(bit)
        if bit == 4:
            (pv,) = call(inner, [shaped((rows, width), F32)], q, keys, values)
            got, pv, grad, by_x, near = phase(got, pv, grad, by_x, near)
        prior.take(bit, got)
    prior = prior.result()

    (o,) = call(outputs, [matrix], prior, queries, pv)
    o, by_x, near, grad = phase(o, by_x, near, grad)
    n = flip(o, "seq", 1)
    far = flip(near, "head", 2)
    by_core, by_xc, near_c = (flip(a, "head", 1) for a in (grad, by_x, near))

    pieces = [out_grad, by_core, by_x, by_xc]
    mine = pieces if short else [half(p, y) for p in pieces]
    (attn_grad,) = call(attn_grad_body, [matrix], out_weight, *pieces)
    (back_term,) = call(state, [state_shape], queries, attn_grad)
    later = Scan(back_term, True)
    got = later.start(2)
    got, n, far = phase(got, n, far)
    far_c = flip(far, "head", 1)
    later.take(2, got)
    operands = (o, n, *mine, near, near_c, far, far_c)

    def gradients(later):
        body = functools.partial(grads_body, scale, part)
        return call(body, [matrix] * 3, queries, keys, values, attn_grad, prior, later)

    if short:
        got = later.start(4)
        pair = (BF16, BF16)
        outs = product((0, 1), (pair, pair), *operands)
        b0, b1 = list(outs[:2]), list(outs[2:])
        e1, e2 = [send(b, OUTER) for b in b0], [send(b1[0], OUTER)]
        o, got, *b0 = phase(o, got, *b0)
        b2, b3 = product((2, 3), ((F32,), (F32,)), o, *operands[1:], cost=1 << 14)
        later.take(4, got)
        got = later.across()
        e1[0], b1[1], got, b2 = phase(e1[0], b1[1], got, b2)
        m2 = [send(add(b0[0], e1[0]), MIDDLE)]
        e2 += [send(b1[1], OUTER)]
        e1[1], m2[0] = phase(e1[1], m2[0])
        m2 += [send(add(b0[1], e1[1], cost=1 << 14), MIDDLE)]
        sent = add(b1[0], e2[0])
        m3 = [send(sent, MIDDLE)]
        m2[1], got, _ = phase(m2[1], got, sent)
        sent = small(joined_body, BF16, b2, *m2)
        e3 = send(sent, OUTER)
        e2[1], _ = phase(e2[1], sent)
        m3 += [send(add(b1[1], e2[1]), MIDDLE)]
        grads = gradients(later.result(got))
        weight_grad = small(total_body, F32, b3, e3, *m3)
    else:
        for bit in later.bits[1:]:
            later.take(bit, later.start(bit))
        grads = gradients(later.result(later.across()))
        groups = [[2 * p + i for p in range(line)] for i in range(2)]
        whole = jnp.concatenate(product(range(n_head), [(F32,)] * n_head, *operands), axis=0)
        weight_grad = lax.psum_scatter(
            whole, "seq", scatter_dimension=0, axis_index_groups=groups, tiled=True
        )
    return (*grads, weight_grad)


def solution(mesh):
    return jax.shard_map(
        per_device,
        mesh=mesh,
        in_specs=(
            P("seq", "head"),
            P("seq", "head"),
            P("seq", "head"),
            P("seq", "head"),
            P(None, "head"),
        ),
        out_specs=(P("seq", "head"), P("seq", "head"), P("seq", "head"), P("seq", "head")),
        check_vma=False,
    )
```

```python
import functools
import math

import jax
import jax.numpy as jnp
from jax import lax
from jax.experimental import pallas as pl
from jax.experimental.pallas import tpu as pltpu
from jax.sharding import PartitionSpec as P

HD = 128
BF16 = jnp.bfloat16
F32 = jnp.float32


def dot(a, b, on_a=1, on_b=0):
    return lax.dot_general(a, b, (((on_a,), (on_b,)), ((), ())), preferred_element_type=F32)


def call(body, outs, *args, scratch=None, cost=1, vmem=12, direct=()):
    scratch = [(a.shape, a.dtype) for a in args] if scratch is None else scratch
    count = len(args)

    def kernel(*refs):
        sources, results = refs[:count], refs[count : len(refs) - len(scratch) - 1]
        buffers, sems = refs[len(refs) - len(scratch) - 1 : -1], refs[-1]
        body(sources, results, buffers, sems)

    return pl.pallas_call(
        kernel,
        out_shape=outs,
        in_specs=[
            pl.BlockSpec(memory_space=pltpu.VMEM if i in direct else pl.ANY) for i in range(count)
        ],
        out_specs=jax.tree.map(lambda _: pl.BlockSpec(memory_space=pltpu.VMEM), outs),
        scratch_shapes=[pltpu.VMEM(*buffer) for buffer in scratch]
        + [pltpu.SemaphoreType.DMA((count + len(scratch),))],
        compiler_params=pltpu.CompilerParams(vmem_limit_bytes=vmem << 20),
        cost_estimate=pl.CostEstimate(flops=cost << 20, bytes_accessed=1 << 14, transcendentals=0),
    )(*args)


def fetch(sources, buffers, sems):
    copies = [
        pltpu.make_async_copy(source, buffer, sems.at[i])
        for i, (source, buffer) in enumerate(zip(sources, buffers))
    ]
    for copy in copies:
        copy.start()

    def wait(i):
        copies[i].wait()
        return buffers[i]

    return wait


def head(h):
    return slice(h * HD, (h + 1) * HD)


def state_body(scale, sources, results, buffers, sems):
    split = None
    if len(sources) > 2:
        width = results[1].shape[1]
        first = (1 - lax.rem(lax.axis_index("seq"), 2)) * width
        half = sources[2].at[:, pl.ds(pl.multiple_of(first, width), width)]
        split = pltpu.make_async_copy(half, results[1], sems.at[len(buffers)])
    wait = fetch(sources[:2], buffers, sems)
    if split is not None:
        split.start()
    a_ref, b_ref = wait(0), wait(1)
    for h in range(a_ref.shape[1] // HD):
        term = dot(a_ref[:, head(h)], b_ref[:, head(h)], 0, 0)
        results[0][head(h), :] = (scale * term).astype(BF16)
    if split is not None:
        split.wait()


def masked(scale, a, b, row):
    scores = scale * dot(a, b, 1, 1)
    rows = row + lax.broadcasted_iota(jnp.int32, scores.shape, 0)
    return jnp.where(lax.broadcasted_iota(jnp.int32, scores.shape, 1) <= rows, scores, 0.0).astype(BF16)


def inner_body(scale, part, sources, results, buffers, sems):
    wait = fetch(sources, buffers, sems)
    q_ref, k_ref, v_ref = wait(0), wait(1), wait(2)
    for h in range(q_ref.shape[1] // HD):
        for row in range(0, q_ref.shape[0], part):
            end = row + part
            probs = masked(scale, q_ref[row:end, head(h)], k_ref[:end, head(h)], row)
            results[0][row:end, head(h)] = dot(probs, v_ref[:end, head(h)])


def outputs_body(sources, results, buffers, sems):
    wait = fetch(sources, buffers, sems)
    prior_ref, q_ref, pv_ref = wait(0), wait(1), wait(2)
    for h in range(q_ref.shape[1] // HD):
        total = pv_ref[:, head(h)] + dot(q_ref[:, head(h)], prior_ref[head(h), :])
        results[0][:, head(h)] = total.astype(BF16)


def attn_grad_body(sources, results, buffers, sems):
    wait = fetch(sources, buffers, sems)
    me = lax.axis_index("head")
    w_ref = wait(0)
    total = None
    for j in range(len(sources) - 1):
        piece = wait(j + 1)
        depth = piece.shape[1]
        rows = pl.ds(pl.multiple_of((me ^ j) * depth, depth), depth)
        term = dot(piece[...], w_ref[rows, :])
        total = term if total is None else total + term
    results[0][...] = total.astype(BF16)


def grads_body(scale, part, sources, results, buffers, sems):
    wait = fetch(sources, buffers, sems)
    q_ref, k_ref, v_ref, d_ref, prior_ref, later_ref = (wait(i) for i in range(6))
    dq_ref, dk_ref, dv_ref = results
    rows = q_ref.shape[0]
    for h in range(q_ref.shape[1] // HD):
        at = head(h)
        dk = dot(v_ref[:, at], later_ref[at, :], 1, 1)
        dv = dot(k_ref[:, at], later_ref[at, :])
        dk_parts = [dk[r : r + part] for r in range(0, rows, part)]
        dv_parts = [dv[r : r + part] for r in range(0, rows, part)]
        for row in range(0, rows, part):
            end = row + part
            q, d = q_ref[row:end, at], d_ref[row:end, at]
            probs = masked(scale, q, k_ref[:end, at], row)
            grads = masked(scale, d, v_ref[:end, at], row)
            dq = dot(grads, k_ref[:end, at]) + dot(d, prior_ref[at, :], 1, 1)
            dq_ref[row:end, at] = dq.astype(BF16)
            for i, r in enumerate(range(0, end, part)):
                dk_parts[i] += dot(grads[:, r : r + part], q, 0, 0)
                dv_parts[i] += dot(probs[:, r : r + part], d, 0, 0)
        for i, r in enumerate(range(0, rows, part)):
            dk_ref[r : r + part, at] = dk_parts[i].astype(BF16)
            dv_ref[r : r + part, at] = dv_parts[i].astype(BF16)


def slot(z, i):
    at = jnp.int32(ORDER[-1][i])
    for p in range(len(ORDER) - 1):
        at = jnp.where(z == p, ORDER[p][i], at)
    return at


def product_body(factor, count, short, slots, parts, sources, results, buffers, sems):
    used = len(slots)
    seq, me = lax.axis_index("seq"), lax.axis_index("head")
    o, n = (pltpu.make_async_copy(sources[i], buffers[i], sems.at[i]) for i in range(2))
    o.start()
    n.start()
    copies = []
    for i, s in enumerate(slots):
        which = (slot(lax.div(seq, 2), s) if short else s) ^ me
        for part in range(2):
            at = 2 + part * used + i
            for j in range(count):

                @pl.when(which == j)
                def _():
                    piece = sources[2 + part * count + j]
                    width = buffers[at].shape[1]
                    if piece.shape[1] != width:
                        first = pl.multiple_of(lax.rem(seq, 2) * width, width)
                        piece = piece.at[:, pl.ds(first, width)]
                    pltpu.make_async_copy(piece, buffers[at], sems.at[at]).start()

            copies.append(pltpu.make_async_copy(buffers[at], buffers[at], sems.at[at]))
    o.wait()
    n.wait()
    results = list(results)
    for i in range(used):
        copies[2 * i].wait()
        copies[2 * i + 1].wait()
        total = dot(buffers[2 + i][...], buffers[0][...], 0, 0)
        total += dot(buffers[2 + used + i][...], buffers[1][...], 0, 0)
        total *= factor
        first = 0
        for _ in range(parts[i]):
            part = results.pop(0)
            part[...] = total[:, first : first + part.shape[1]].astype(part.dtype)
            first += part.shape[1]


def first_body(factor, count, loaded, sources, results, buffers, sems):
    seq, me = lax.axis_index("seq"), lax.axis_index("head")
    which = slot(lax.div(seq, 2), 0) ^ me
    for j in range(count):

        @pl.when(which == j)
        def _():
            piece = sources[1 + j]
            width = buffers[0].shape[1]
            if piece.shape[1] != width:
                first = pl.multiple_of(lax.rem(seq, 2) * width, width)
                piece = piece.at[:, pl.ds(first, width)]
            pltpu.make_async_copy(piece, buffers[0], sems.at[0]).start()

    o_ref = sources[0]
    if loaded:
        load = pltpu.make_async_copy(o_ref, buffers[1], sems.at[1])
        load.start()
        load.wait()
        o_ref = buffers[1]
    pltpu.make_async_copy(buffers[0], buffers[0], sems.at[0]).wait()
    total = factor * dot(buffers[0][...], o_ref[...], 0, 0)
    if len(sources) > count + 1:
        total += sources[-1][...]
    first = 0
    for out in results:
        out[...] = total[:, first : first + out.shape[1]].astype(out.dtype)
        first += out.shape[1]


def phase(*values):
    return lax.optimization_barrier(values)


def flip(a, axis, bit):
    return lax.ppermute(a, axis, [(i, i ^ bit) for i in range(lax.axis_size(axis))])


def add_body(*refs):
    *sources, out = refs
    out[...] = sum(ref[...].astype(F32) for ref in sources).astype(out.dtype)


def add(*terms, kind=BF16, cost=1):
    spec = pl.BlockSpec(memory_space=pltpu.VMEM)
    return pl.pallas_call(
        add_body,
        out_shape=jax.ShapeDtypeStruct(terms[0].shape, kind),
        in_specs=[spec] * len(terms),
        out_specs=spec,
        compiler_params=pltpu.CompilerParams(vmem_limit_bytes=8 << 20),
        cost_estimate=pl.CostEstimate(flops=cost << 20, bytes_accessed=1 << 14, transcendentals=0),
    )(*terms)


def total_body(front_ref, back_ref, m_ref, e_ref, out_ref):
    width = front_ref.shape[1]
    out_ref[:, :width] = front_ref[...]
    out_ref[:, width:] = back_ref[...] + m_ref[...].astype(F32) + e_ref[...].astype(F32)


def small(body, kind, *terms, wide=1):
    spec = pl.BlockSpec(memory_space=pltpu.VMEM)
    return pl.pallas_call(
        body,
        out_shape=jax.ShapeDtypeStruct((terms[0].shape[0], terms[0].shape[1] * wide), kind),
        in_specs=[spec] * len(terms),
        out_specs=spec,
        compiler_params=pltpu.CompilerParams(vmem_limit_bytes=8 << 20),
        cost_estimate=pl.CostEstimate(flops=1 << 20, bytes_accessed=1 << 14, transcendentals=0),
    )(*terms)


class Scan:
    def __init__(self, term, later):
        self.term, self.later, self.total, self.before = term, later, term, 0.0
        self.bits = [1 << i for i in range(lax.axis_size("seq").bit_length() - 1)]

    def inside(self, bit):
        return ((lax.axis_index("seq") & bit) != 0) != self.later

    def start(self, bit):
        return flip(self.total, "seq", bit)

    def take(self, bit, got):
        self.before += jnp.where(self.inside(bit), got, 0).astype(F32)
        self.total = add(self.total, got)

    def across(self):
        own = jnp.where(self.inside(1), 0, self.term).astype(F32)
        return flip((self.before + own).astype(BF16), "seq", 1)

    def result(self, got=0.0):
        return (self.before + got).astype(BF16)


def send(a, pairs):
    return lax.ppermute(a, "seq", [(2 * s + i, 2 * t + i) for s, t in pairs for i in range(2)])


OUTER = ((0, 1), (1, 0), (2, 3), (3, 2))
MIDDLE = ((1, 2), (2, 1))
ORDER = ((3, 2, 1, 0), (3, 2, 0, 1), (0, 1, 3, 2), (0, 1, 2, 3))


def per_device(queries, keys, values, out_grad, out_weight):
    rows, width = queries.shape
    n_seq, n_head = lax.axis_size("seq"), lax.axis_size("head")
    seq = lax.axis_index("seq")
    y = seq % 2
    line = n_seq // 2
    total = n_seq * rows
    scale = 1.0 / math.sqrt(HD * total)
    factor = 1.0 / math.sqrt(total)
    part = 256
    shaped = lambda dims, dtype=BF16: jax.ShapeDtypeStruct(dims, dtype)
    state = functools.partial(state_body, scale)
    state_shape = shaped((width, HD))

    cols = out_grad.shape[1]
    block = cols * n_head // n_seq
    short = line == 4 and n_head == 4

    def half(a, i):
        cut = a.reshape(rows, cols // (2 * block), 2, block)
        return lax.dynamic_index_in_dim(cut, i, 2, keepdims=False).reshape(rows, cols // 2)

    inner = functools.partial(inner_body, scale, part)
    outputs = outputs_body
    matrix = shaped((rows, width))

    def product(slots, kinds, *operands, cost=1):
        body = functools.partial(product_body, factor, n_head, short, slots, [len(k) for k in kinds])
        outs = [shaped((cols // 2, width // len(k)), kind) for k in kinds for kind in k]
        like = [((rows, cols // 2), BF16)] * (2 * len(slots))
        scratch = [((rows, width), BF16)] * 2 + like
        return call(body, outs, *operands, scratch=scratch, cost=cost, vmem=60)

    by_x = flip(out_grad, "head", 2)
    if short:
        scratch = [((rows, width), BF16)] * 2
        outs = [state_shape, shaped((rows, cols // 2))]
        kv_term, other = call(state, outs, keys, values, out_grad, scratch=scratch, vmem=60)
    else:
        (kv_term,), other = call(state, [state_shape], keys, values), half(out_grad, 1 - y)
    prior = Scan(kv_term, False)
    got = prior.start(1)
    got, other, q, grad = phase(got, other, queries, out_grad)
    near = flip(other, "seq", 1)
    prior.take(1, got)
    for bit in prior.bits[1:]:
        got = prior.start(bit)
        if bit == 4:
            (pv,) = call(inner, [shaped((rows, width), F32)], q, keys, values)
            got, pv, grad, by_x, near = phase(got, pv, grad, by_x, near)
        prior.take(bit, got)
    prior = prior.result()

    (o,) = call(outputs, [matrix], prior, queries, pv)
    o, by_x, near, grad = phase(o, by_x, near, grad)
    n = flip(o, "seq", 1)
    far = flip(near, "head", 2)
    by_core, by_xc, near_c = (flip(a, "head", 1) for a in (grad, by_x, near))

    pieces = [out_grad, by_core, by_x, by_xc]
    mine = pieces if short else [half(p, y) for p in pieces]
    (attn_grad,) = call(attn_grad_body, [matrix], out_weight, *pieces)
    (back_term,) = call(state, [state_shape], queries, attn_grad)
    later = Scan(back_term, True)
    got = later.start(2)
    if short:
        first = functools.partial(first_body, factor, n_head)
        scratch = [((rows, cols // 2), BF16), ((rows, width), BF16)]
        outs = [shaped((cols // 2, width), F32)]
        o, _ = phase(o, back_term)
        (begun,) = call(functools.partial(first, True), outs, o, *mine, scratch=scratch, vmem=60)
        got, n, far, begun = phase(got, n, far, begun)
    else:
        got, n, far = phase(got, n, far)
    far_c = flip(far, "head", 1)
    later.take(2, got)
    operands = (o, n, *mine, near, near_c, far, far_c)

    def gradients(later):
        body = functools.partial(grads_body, scale, part)
        return call(body, [matrix] * 3, queries, keys, values, attn_grad, prior, later)

    if short:
        got = later.start(4)
        pair = (BF16, BF16)
        outs = [shaped((cols // 2, width // 2))] * 2
        theirs = (near, near_c, far, far_c)
        first = functools.partial(first, False)
        b0 = call(first, outs, n, *theirs, begun, scratch=scratch[:1], vmem=8, direct=(0, n_head + 1))
        e1 = [send(b, OUTER) for b in b0]
        o, got, *b0 = phase(o, got, *b0)
        outs = product((1, 2, 3), (pair, (F32, F32), (F32, F32)), o, *operands[1:], cost=1 << 14)
        b1, b2, (b3, b3_back) = list(outs[:2]), outs[2:4], outs[4:]
        e2 = [send(b1[0], OUTER)]
        later.take(4, got)
        got = later.across()
        e1[0], b1[1], got, *b2 = phase(e1[0], b1[1], got, *b2)
        m2 = [send(add(b0[0], e1[0]), MIDDLE)]
        e2 += [send(b1[1], OUTER)]
        m2 += [send(add(b0[1], e1[1], cost=1024), MIDDLE)]
        e2[0], m2[0] = phase(e2[0], m2[0])
        sent = add(b1[0], e2[0], cost=2048)
        m3 = [send(sent, MIDDLE)]
        m2[1], got, _ = phase(m2[1], got, sent)
        parts = [add(b, m) for b, m in zip(b2, m2)]
        e3 = [send(p, OUTER) for p in parts]
        e2[1], _, _ = phase(e2[1], *parts)
        m3 += [send(add(b1[1], e2[1]), MIDDLE)]
        grads = gradients(later.result(got))
        front = add(b3, m3[0], e3[0], kind=F32, cost=2048)
        weight_grad = small(total_body, F32, front, b3_back, m3[1], e3[1], wide=2)
    else:
        for bit in later.bits[1:]:
            later.take(bit, later.start(bit))
        grads = gradients(later.result(later.across()))
        groups = [[2 * p + i for p in range(line)] for i in range(2)]
        whole = jnp.concatenate(product(range(n_head), [(F32,)] * n_head, *operands), axis=0)
        weight_grad = lax.psum_scatter(
            whole, "seq", scatter_dimension=0, axis_index_groups=groups, tiled=True
        )
    return (*grads, weight_grad)


def solution(mesh):
    return jax.shard_map(
        per_device,
        mesh=mesh,
        in_specs=(
            P("seq", "head"),
            P("seq", "head"),
            P("seq", "head"),
            P("seq", "head"),
            P(None, "head"),
        ),
        out_specs=(P("seq", "head"), P("seq", "head"), P("seq", "head"), P("seq", "head")),
        check_vma=False,
    )
```

```python
import functools
import math

import jax
import jax.numpy as jnp
from jax import lax
from jax.experimental import pallas as pl
from jax.experimental.pallas import tpu as pltpu
from jax.sharding import PartitionSpec as P

HD = 128
BF16 = jnp.bfloat16
F32 = jnp.float32


def dot(a, b, on_a=1, on_b=0):
    return lax.dot_general(a, b, (((on_a,), (on_b,)), ((), ())), preferred_element_type=F32)


def call(body, outs, *args, scratch=None, cost=1, vmem=12, direct=()):
    scratch = [(a.shape, a.dtype) for a in args] if scratch is None else scratch
    count = len(args)

    def kernel(*refs):
        sources, results = refs[:count], refs[count : len(refs) - len(scratch) - 1]
        buffers, sems = refs[len(refs) - len(scratch) - 1 : -1], refs[-1]
        body(sources, results, buffers, sems)

    return pl.pallas_call(
        kernel,
        out_shape=outs,
        in_specs=[
            pl.BlockSpec(memory_space=pltpu.VMEM if i in direct else pl.ANY) for i in range(count)
        ],
        out_specs=jax.tree.map(lambda _: pl.BlockSpec(memory_space=pltpu.VMEM), outs),
        scratch_shapes=[pltpu.VMEM(*buffer) for buffer in scratch]
        + [pltpu.SemaphoreType.DMA((count + len(scratch),))],
        compiler_params=pltpu.CompilerParams(vmem_limit_bytes=vmem << 20),
        cost_estimate=pl.CostEstimate(flops=cost << 20, bytes_accessed=1 << 14, transcendentals=0),
    )(*args)


def fetch(sources, buffers, sems):
    copies = [
        pltpu.make_async_copy(source, buffer, sems.at[i])
        for i, (source, buffer) in enumerate(zip(sources, buffers))
    ]
    for copy in copies:
        copy.start()

    def wait(i):
        copies[i].wait()
        return buffers[i]

    return wait


def head(h):
    return slice(h * HD, (h + 1) * HD)


def state_body(scale, sources, results, buffers, sems):
    split = None
    if len(sources) > 2:
        width = results[1].shape[1]
        first = (1 - lax.rem(lax.axis_index("seq"), 2)) * width
        half = sources[2].at[:, pl.ds(pl.multiple_of(first, width), width)]
        split = pltpu.make_async_copy(half, results[1], sems.at[len(buffers)])
    wait = fetch(sources[:2], buffers, sems)
    if split is not None:
        split.start()
    a_ref, b_ref = wait(0), wait(1)
    for h in range(a_ref.shape[1] // HD):
        term = dot(a_ref[:, head(h)], b_ref[:, head(h)], 0, 0)
        results[0][head(h), :] = (scale * term).astype(BF16)
    if split is not None:
        split.wait()


def masked(scale, a, b, row):
    scores = scale * dot(a, b, 1, 1)
    rows = row + lax.broadcasted_iota(jnp.int32, scores.shape, 0)
    return jnp.where(lax.broadcasted_iota(jnp.int32, scores.shape, 1) <= rows, scores, 0.0).astype(BF16)


def inner_body(scale, part, sources, results, buffers, sems):
    wait = fetch(sources, buffers, sems)
    q_ref, k_ref, v_ref = wait(0), wait(1), wait(2)
    for h in range(q_ref.shape[1] // HD):
        for row in range(0, q_ref.shape[0], part):
            end = row + part
            probs = masked(scale, q_ref[row:end, head(h)], k_ref[:end, head(h)], row)
            results[0][row:end, head(h)] = dot(probs, v_ref[:end, head(h)])


def outputs_body(sources, results, buffers, sems):
    wait = fetch(sources, buffers, sems)
    prior_ref, q_ref, pv_ref = wait(0), wait(1), wait(2)
    for h in range(q_ref.shape[1] // HD):
        total = pv_ref[:, head(h)] + dot(q_ref[:, head(h)], prior_ref[head(h), :])
        results[0][:, head(h)] = total.astype(BF16)


def attn_grad_body(sources, results, buffers, sems):
    wait = fetch(sources, buffers, sems)
    me = lax.axis_index("head")
    w_ref = wait(0)
    total = None
    for j in range(len(sources) - 1):
        piece = wait(j + 1)
        depth = piece.shape[1]
        rows = pl.ds(pl.multiple_of((me ^ j) * depth, depth), depth)
        term = dot(piece[...], w_ref[rows, :])
        total = term if total is None else total + term
    results[0][...] = total.astype(BF16)


def grads_body(scale, part, sources, results, buffers, sems):
    wait = fetch(sources, buffers, sems)
    q_ref, k_ref, v_ref, d_ref, prior_ref, later_ref = (wait(i) for i in range(6))
    dq_ref, dk_ref, dv_ref = results
    rows = q_ref.shape[0]
    for h in range(q_ref.shape[1] // HD):
        at = head(h)
        dk = dot(v_ref[:, at], later_ref[at, :], 1, 1)
        dv = dot(k_ref[:, at], later_ref[at, :])
        dk_parts = [dk[r : r + part] for r in range(0, rows, part)]
        dv_parts = [dv[r : r + part] for r in range(0, rows, part)]
        for row in range(0, rows, part):
            end = row + part
            q, d = q_ref[row:end, at], d_ref[row:end, at]
            probs = masked(scale, q, k_ref[:end, at], row)
            grads = masked(scale, d, v_ref[:end, at], row)
            dq = dot(grads, k_ref[:end, at]) + dot(d, prior_ref[at, :], 1, 1)
            dq_ref[row:end, at] = dq.astype(BF16)
            for i, r in enumerate(range(0, end, part)):
                dk_parts[i] += dot(grads[:, r : r + part], q, 0, 0)
                dv_parts[i] += dot(probs[:, r : r + part], d, 0, 0)
        for i, r in enumerate(range(0, rows, part)):
            dk_ref[r : r + part, at] = dk_parts[i].astype(BF16)
            dv_ref[r : r + part, at] = dv_parts[i].astype(BF16)


def slot(z, i):
    at = jnp.int32(ORDER[-1][i])
    for p in range(len(ORDER) - 1):
        at = jnp.where(z == p, ORDER[p][i], at)
    return at


def product_body(factor, count, short, slots, parts, sources, results, buffers, sems):
    used = len(slots)
    seq, me = lax.axis_index("seq"), lax.axis_index("head")
    o, n = (pltpu.make_async_copy(sources[i], buffers[i], sems.at[i]) for i in range(2))
    o.start()
    n.start()
    copies = []
    for i, s in enumerate(slots):
        which = (slot(lax.div(seq, 2), s) if short else s) ^ me
        for part in range(2):
            at = 2 + part * used + i
            for j in range(count):

                @pl.when(which == j)
                def _():
                    piece = sources[2 + part * count + j]
                    width = buffers[at].shape[1]
                    if piece.shape[1] != width:
                        first = pl.multiple_of(lax.rem(seq, 2) * width, width)
                        piece = piece.at[:, pl.ds(first, width)]
                    pltpu.make_async_copy(piece, buffers[at], sems.at[at]).start()

            copies.append(pltpu.make_async_copy(buffers[at], buffers[at], sems.at[at]))
    o.wait()
    n.wait()
    results = list(results)
    for i in range(used):
        copies[2 * i].wait()
        copies[2 * i + 1].wait()
        total = dot(buffers[2 + i][...], buffers[0][...], 0, 0)
        total += dot(buffers[2 + used + i][...], buffers[1][...], 0, 0)
        total *= factor
        first = 0
        for _ in range(parts[i]):
            part = results.pop(0)
            part[...] = total[:, first : first + part.shape[1]].astype(part.dtype)
            first += part.shape[1]


def first_body(factor, count, loaded, sources, results, buffers, sems):
    seq, me = lax.axis_index("seq"), lax.axis_index("head")
    which = slot(lax.div(seq, 2), 0) ^ me
    for j in range(count):

        @pl.when(which == j)
        def _():
            piece = sources[1 + j]
            width = buffers[0].shape[1]
            if piece.shape[1] != width:
                first = pl.multiple_of(lax.rem(seq, 2) * width, width)
                piece = piece.at[:, pl.ds(first, width)]
            pltpu.make_async_copy(piece, buffers[0], sems.at[0]).start()

    o_ref = sources[0]
    if loaded:
        load = pltpu.make_async_copy(o_ref, buffers[1], sems.at[1])
        load.start()
        load.wait()
        o_ref = buffers[1]
    pltpu.make_async_copy(buffers[0], buffers[0], sems.at[0]).wait()
    total = factor * dot(buffers[0][...], o_ref[...], 0, 0)
    if len(sources) > count + 1:
        total += sources[-1][...]
    first = 0
    for out in results:
        out[...] = total[:, first : first + out.shape[1]].astype(out.dtype)
        first += out.shape[1]


def phase(*values):
    return lax.optimization_barrier(values)


def flip(a, axis, bit):
    return lax.ppermute(a, axis, [(i, i ^ bit) for i in range(lax.axis_size(axis))])


def add_body(*refs):
    *sources, out = refs
    out[...] = sum(ref[...].astype(F32) for ref in sources).astype(out.dtype)


def add(*terms, kind=BF16, cost=1):
    spec = pl.BlockSpec(memory_space=pltpu.VMEM)
    return pl.pallas_call(
        add_body,
        out_shape=jax.ShapeDtypeStruct(terms[0].shape, kind),
        in_specs=[spec] * len(terms),
        out_specs=spec,
        compiler_params=pltpu.CompilerParams(vmem_limit_bytes=8 << 20),
        cost_estimate=pl.CostEstimate(flops=cost << 20, bytes_accessed=1 << 14, transcendentals=0),
    )(*terms)


def half_body(first, *refs):
    *sources, out_ref, sum_ref, sem = refs
    sources = sources[-3:]
    sum_ref[...] = sum(ref[...].astype(F32) for ref in sources)
    columns = out_ref.at[:, pl.ds(first, sum_ref.shape[1])]
    copy = pltpu.make_async_copy(sum_ref, columns, sem)
    copy.start()
    copy.wait()


def half_sum(first, width, out, *terms, cost=1):
    rows, part = terms[0].shape
    spec = pl.BlockSpec(memory_space=pltpu.VMEM)
    whole = pl.BlockSpec(memory_space=pl.ANY)
    operands = terms if out is None else (out, *terms)
    return pl.pallas_call(
        functools.partial(half_body, first),
        out_shape=jax.ShapeDtypeStruct((rows, width), F32),
        in_specs=([] if out is None else [whole]) + [spec] * len(terms),
        out_specs=whole,
        scratch_shapes=[pltpu.VMEM((rows, part), F32), pltpu.SemaphoreType.DMA],
        input_output_aliases={} if out is None else {0: 0},
        compiler_params=pltpu.CompilerParams(vmem_limit_bytes=8 << 20),
        cost_estimate=pl.CostEstimate(flops=cost << 20, bytes_accessed=1 << 14, transcendentals=0),
    )(*operands)


def small(body, kind, *terms, wide=1):
    spec = pl.BlockSpec(memory_space=pltpu.VMEM)
    return pl.pallas_call(
        body,
        out_shape=jax.ShapeDtypeStruct((terms[0].shape[0], terms[0].shape[1] * wide), kind),
        in_specs=[spec] * len(terms),
        out_specs=spec,
        compiler_params=pltpu.CompilerParams(vmem_limit_bytes=8 << 20),
        cost_estimate=pl.CostEstimate(flops=1 << 20, bytes_accessed=1 << 14, transcendentals=0),
    )(*terms)


class Scan:
    def __init__(self, term, later):
        self.term, self.later, self.total, self.before = term, later, term, 0.0
        self.bits = [1 << i for i in range(lax.axis_size("seq").bit_length() - 1)]

    def inside(self, bit):
        return ((lax.axis_index("seq") & bit) != 0) != self.later

    def start(self, bit):
        return flip(self.total, "seq", bit)

    def take(self, bit, got):
        self.before += jnp.where(self.inside(bit), got, 0).astype(F32)
        self.total = add(self.total, got)

    def across(self):
        own = jnp.where(self.inside(1), 0, self.term).astype(F32)
        return flip((self.before + own).astype(BF16), "seq", 1)

    def result(self, got=0.0):
        return (self.before + got).astype(BF16)


def send(a, pairs):
    return lax.ppermute(a, "seq", [(2 * s + i, 2 * t + i) for s, t in pairs for i in range(2)])


OUTER = ((0, 1), (1, 0), (2, 3), (3, 2))
MIDDLE = ((1, 2), (2, 1))
ORDER = ((3, 2, 1, 0), (3, 2, 0, 1), (0, 1, 3, 2), (0, 1, 2, 3))


def per_device(queries, keys, values, out_grad, out_weight):
    rows, width = queries.shape
    n_seq, n_head = lax.axis_size("seq"), lax.axis_size("head")
    seq = lax.axis_index("seq")
    y = seq % 2
    line = n_seq // 2
    total = n_seq * rows
    scale = 1.0 / math.sqrt(HD * total)
    factor = 1.0 / math.sqrt(total)
    part = 256
    shaped = lambda dims, dtype=BF16: jax.ShapeDtypeStruct(dims, dtype)
    state = functools.partial(state_body, scale)
    state_shape = shaped((width, HD))

    cols = out_grad.shape[1]
    block = cols * n_head // n_seq
    short = line == 4 and n_head == 4

    def half(a, i):
        cut = a.reshape(rows, cols // (2 * block), 2, block)
        return lax.dynamic_index_in_dim(cut, i, 2, keepdims=False).reshape(rows, cols // 2)

    inner = functools.partial(inner_body, scale, part)
    outputs = outputs_body
    matrix = shaped((rows, width))

    def product(slots, kinds, *operands, cost=1):
        body = functools.partial(product_body, factor, n_head, short, slots, [len(k) for k in kinds])
        outs = [shaped((cols // 2, width // len(k)), kind) for k in kinds for kind in k]
        like = [((rows, cols // 2), BF16)] * (2 * len(slots))
        scratch = [((rows, width), BF16)] * 2 + like
        return call(body, outs, *operands, scratch=scratch, cost=cost, vmem=60)

    by_x = flip(out_grad, "head", 2)
    if short:
        scratch = [((rows, width), BF16)] * 2
        outs = [state_shape, shaped((rows, cols // 2))]
        kv_term, other = call(state, outs, keys, values, out_grad, scratch=scratch, vmem=60)
    else:
        (kv_term,), other = call(state, [state_shape], keys, values), half(out_grad, 1 - y)
    prior = Scan(kv_term, False)
    got = prior.start(1)
    got, other, q, grad = phase(got, other, queries, out_grad)
    near = flip(other, "seq", 1)
    by_core = flip(grad, "head", 1)
    prior.take(1, got)
    for bit in prior.bits[1:]:
        got = prior.start(bit)
        if bit == 4:
            (pv,) = call(inner, [shaped((rows, width), F32)], q, keys, values)
            got, pv, grad, by_x, near = phase(got, pv, grad, by_x, near)
        prior.take(bit, got)
    prior = prior.result()

    (o,) = call(outputs, [matrix], prior, queries, pv)
    o, by_x, near = phase(o, by_x, near)
    n = flip(o, "seq", 1)
    far = flip(near, "head", 2)
    by_xc = flip(by_x, "head", 1)

    pieces = [out_grad, by_core, by_x, by_xc]
    mine = pieces if short else [half(p, y) for p in pieces]
    (attn_grad,) = call(attn_grad_body, [matrix], out_weight, *pieces)
    (back_term,) = call(state, [state_shape], queries, attn_grad)
    later = Scan(back_term, True)
    got = later.start(2)
    if short:
        first = functools.partial(first_body, factor, n_head)
        scratch = [((rows, cols // 2), BF16), ((rows, width), BF16)]
        outs = [shaped((cols // 2, width), F32)]
        o, near, back_term = phase(o, near, back_term)
        near_c = flip(near, "head", 1)
        (begun,) = call(functools.partial(first, True), outs, o, *mine, scratch=scratch, vmem=60)
        got, n, far, begun = phase(got, n, far, begun)
    else:
        near_c = flip(near, "head", 1)
        got, n, far = phase(got, n, far)
    far_c = flip(far, "head", 1)
    later.take(2, got)
    operands = (o, n, *mine, near, near_c, far, far_c)

    def gradients(later):
        body = functools.partial(grads_body, scale, part)
        return call(body, [matrix] * 3, queries, keys, values, attn_grad, prior, later)

    if short:
        got = later.start(4)
        pair = (BF16, BF16)
        outs = [shaped((cols // 2, width // 2))] * 2
        theirs = (near, near_c, far, far_c)
        first = functools.partial(first, False)
        b0 = call(first, outs, n, *theirs, begun, scratch=scratch[:1], vmem=8, direct=(0, n_head + 1))
        e1 = [send(b, OUTER) for b in b0]
        o, got, *b0 = phase(o, got, *b0)
        outs = product((1, 2, 3), (pair, (F32, F32), (F32, F32)), o, *operands[1:], cost=1 << 14)
        b1, b2, (b3, b3_back) = list(outs[:2]), outs[2:4], outs[4:]
        e2 = [send(b1[0], OUTER)]
        later.take(4, got)
        got = later.across()
        e1[0], b1[1], got, *b2 = phase(e1[0], b1[1], got, *b2)
        m2 = [send(add(b0[0], e1[0]), MIDDLE)]
        e2 += [send(b1[1], OUTER)]
        m2 += [send(add(b0[1], e1[1], cost=1024), MIDDLE)]
        e2[0], m2[0] = phase(e2[0], m2[0])
        sent = add(b1[0], e2[0], cost=2048)
        m3 = [send(sent, MIDDLE)]
        m2[1], got, _ = phase(m2[1], got, sent)
        parts = [add(b, m) for b, m in zip(b2, m2)]
        e3 = [send(p, OUTER) for p in parts]
        e2[1], _, _ = phase(e2[1], *parts)
        m3 += [send(add(b1[1], e2[1]), MIDDLE)]
        grads = gradients(later.result(got))
        weight_grad = half_sum(0, width, None, b3, m3[0], e3[0], cost=2048)
        weight_grad = half_sum(width // 2, width, weight_grad, b3_back, m3[1], e3[1])
    else:
        for bit in later.bits[1:]:
            later.take(bit, later.start(bit))
        grads = gradients(later.result(later.across()))
        groups = [[2 * p + i for p in range(line)] for i in range(2)]
        whole = jnp.concatenate(product(range(n_head), [(F32,)] * n_head, *operands), axis=0)
        weight_grad = lax.psum_scatter(
            whole, "seq", scatter_dimension=0, axis_index_groups=groups, tiled=True
        )
    return (*grads, weight_grad)


def solution(mesh):
    return jax.shard_map(
        per_device,
        mesh=mesh,
        in_specs=(
            P("seq", "head"),
            P("seq", "head"),
            P("seq", "head"),
            P("seq", "head"),
            P(None, "head"),
        ),
        out_specs=(P("seq", "head"), P("seq", "head"), P("seq", "head"), P("seq", "head")),
        check_vma=False,
    )
```

```python
import functools
import math

import jax
import jax.numpy as jnp
from jax import lax
from jax.experimental import pallas as pl
from jax.experimental.pallas import tpu as pltpu
from jax.sharding import PartitionSpec as P

HD = 128
BF16 = jnp.bfloat16
F32 = jnp.float32


def dot(a, b, on_a=1, on_b=0):
    return lax.dot_general(a, b, (((on_a,), (on_b,)), ((), ())), preferred_element_type=F32)


def call(body, outs, *args, scratch=None, cost=1, vmem=12, direct=()):
    scratch = [(a.shape, a.dtype) for a in args] if scratch is None else scratch
    count = len(args)

    def kernel(*refs):
        sources, results = refs[:count], refs[count : len(refs) - len(scratch) - 1]
        buffers, sems = refs[len(refs) - len(scratch) - 1 : -1], refs[-1]
        body(sources, results, buffers, sems)

    return pl.pallas_call(
        kernel,
        out_shape=outs,
        in_specs=[
            pl.BlockSpec(memory_space=pltpu.VMEM if i in direct else pl.ANY) for i in range(count)
        ],
        out_specs=jax.tree.map(lambda _: pl.BlockSpec(memory_space=pltpu.VMEM), outs),
        scratch_shapes=[pltpu.VMEM(*buffer) for buffer in scratch]
        + [pltpu.SemaphoreType.DMA((count + len(scratch),))],
        compiler_params=pltpu.CompilerParams(vmem_limit_bytes=vmem << 20),
        cost_estimate=pl.CostEstimate(flops=cost << 20, bytes_accessed=1 << 14, transcendentals=0),
    )(*args)


def fetch(sources, buffers, sems):
    copies = [
        pltpu.make_async_copy(source, buffer, sems.at[i])
        for i, (source, buffer) in enumerate(zip(sources, buffers))
    ]
    for copy in copies:
        copy.start()

    def wait(i):
        copies[i].wait()
        return buffers[i]

    return wait


def head(h):
    return slice(h * HD, (h + 1) * HD)


def state_body(scale, sources, results, buffers, sems):
    split = None
    if len(sources) > 2:
        width = results[1].shape[1]
        first = (1 - lax.rem(lax.axis_index("seq"), 2)) * width
        half = sources[2].at[:, pl.ds(pl.multiple_of(first, width), width)]
        split = pltpu.make_async_copy(half, results[1], sems.at[len(buffers)])
    wait = fetch(sources[:2], buffers, sems)
    if split is not None:
        split.start()
    a_ref, b_ref = wait(0), wait(1)
    for h in range(a_ref.shape[1] // HD):
        term = dot(a_ref[:, head(h)], b_ref[:, head(h)], 0, 0)
        results[0][head(h), :] = (scale * term).astype(BF16)
    if split is not None:
        split.wait()


def masked(scale, a, b, row):
    scores = scale * dot(a, b, 1, 1)
    rows = row + lax.broadcasted_iota(jnp.int32, scores.shape, 0)
    return jnp.where(lax.broadcasted_iota(jnp.int32, scores.shape, 1) <= rows, scores, 0.0).astype(BF16)


def inner_body(scale, part, sources, results, buffers, sems):
    wait = fetch(sources, buffers, sems)
    q_ref, k_ref, v_ref = wait(0), wait(1), wait(2)
    for h in range(q_ref.shape[1] // HD):
        for row in range(0, q_ref.shape[0], part):
            end = row + part
            probs = masked(scale, q_ref[row:end, head(h)], k_ref[:end, head(h)], row)
            results[0][row:end, head(h)] = dot(probs, v_ref[:end, head(h)])


def outputs_body(sources, results, buffers, sems):
    wait = fetch(sources, buffers, sems)
    prior_ref, q_ref, pv_ref = wait(0), wait(1), wait(2)
    for h in range(q_ref.shape[1] // HD):
        total = pv_ref[:, head(h)] + dot(q_ref[:, head(h)], prior_ref[head(h), :])
        results[0][:, head(h)] = total.astype(BF16)


def attn_grad_body(sources, results, buffers, sems):
    wait = fetch(sources, buffers, sems)
    me = lax.axis_index("head")
    w_ref = wait(0)
    total = None
    for j in range(len(sources) - 1):
        piece = wait(j + 1)
        depth = piece.shape[1]
        rows = pl.ds(pl.multiple_of((me ^ j) * depth, depth), depth)
        term = dot(piece[...], w_ref[rows, :])
        total = term if total is None else total + term
    results[0][...] = total.astype(BF16)


def grads_body(scale, part, sources, results, buffers, sems):
    wait = fetch(sources, buffers, sems)
    q_ref, k_ref, v_ref, d_ref, prior_ref, later_ref = (wait(i) for i in range(6))
    dq_ref, dk_ref, dv_ref = results
    rows = q_ref.shape[0]
    for h in range(q_ref.shape[1] // HD):
        at = head(h)
        dk = dot(v_ref[:, at], later_ref[at, :], 1, 1)
        dv = dot(k_ref[:, at], later_ref[at, :])
        dk_parts = [dk[r : r + part] for r in range(0, rows, part)]
        dv_parts = [dv[r : r + part] for r in range(0, rows, part)]
        for row in range(0, rows, part):
            end = row + part
            q, d = q_ref[row:end, at], d_ref[row:end, at]
            probs = masked(scale, q, k_ref[:end, at], row)
            grads = masked(scale, d, v_ref[:end, at], row)
            dq = dot(grads, k_ref[:end, at]) + dot(d, prior_ref[at, :], 1, 1)
            dq_ref[row:end, at] = dq.astype(BF16)
            for i, r in enumerate(range(0, end, part)):
                dk_parts[i] += dot(grads[:, r : r + part], q, 0, 0)
                dv_parts[i] += dot(probs[:, r : r + part], d, 0, 0)
        for i, r in enumerate(range(0, rows, part)):
            dk_ref[r : r + part, at] = dk_parts[i].astype(BF16)
            dv_ref[r : r + part, at] = dv_parts[i].astype(BF16)


def slot(z, i):
    at = jnp.int32(ORDER[-1][i])
    for p in range(len(ORDER) - 1):
        at = jnp.where(z == p, ORDER[p][i], at)
    return at


def product_body(factor, count, short, slots, parts, sources, results, buffers, sems):
    used = len(slots)
    seq, me = lax.axis_index("seq"), lax.axis_index("head")
    o, n = (pltpu.make_async_copy(sources[i], buffers[i], sems.at[i]) for i in range(2))
    o.start()
    n.start()
    copies = []
    for i, s in enumerate(slots):
        which = (slot(lax.div(seq, 2), s) if short else s) ^ me
        for part in range(2):
            at = 2 + part * used + i
            for j in range(count):

                @pl.when(which == j)
                def _():
                    piece = sources[2 + part * count + j]
                    width = buffers[at].shape[1]
                    if piece.shape[1] != width:
                        first = pl.multiple_of(lax.rem(seq, 2) * width, width)
                        piece = piece.at[:, pl.ds(first, width)]
                    pltpu.make_async_copy(piece, buffers[at], sems.at[at]).start()

            copies.append(pltpu.make_async_copy(buffers[at], buffers[at], sems.at[at]))
    o.wait()
    n.wait()
    results = list(results)
    for i in range(used):
        copies[2 * i].wait()
        copies[2 * i + 1].wait()
        total = dot(buffers[2 + i][...], buffers[0][...], 0, 0)
        total += dot(buffers[2 + used + i][...], buffers[1][...], 0, 0)
        total *= factor
        first = 0
        for _ in range(parts[i]):
            part = results.pop(0)
            part[...] = total[:, first : first + part.shape[1]].astype(part.dtype)
            first += part.shape[1]


def first_body(factor, count, loaded, sources, results, buffers, sems):
    seq, me = lax.axis_index("seq"), lax.axis_index("head")
    which = slot(lax.div(seq, 2), 0) ^ me
    for j in range(count):

        @pl.when(which == j)
        def _():
            piece = sources[1 + j]
            width = buffers[0].shape[1]
            if piece.shape[1] != width:
                first = pl.multiple_of(lax.rem(seq, 2) * width, width)
                piece = piece.at[:, pl.ds(first, width)]
            pltpu.make_async_copy(piece, buffers[0], sems.at[0]).start()

    o_ref = sources[0]
    if loaded:
        load = pltpu.make_async_copy(o_ref, buffers[1], sems.at[1])
        load.start()
        load.wait()
        o_ref = buffers[1]
    pltpu.make_async_copy(buffers[0], buffers[0], sems.at[0]).wait()
    total = factor * dot(buffers[0][...], o_ref[...], 0, 0)
    if len(sources) > count + 1:
        total += sources[-1][...]
    first = 0
    for out in results:
        out[...] = total[:, first : first + out.shape[1]].astype(out.dtype)
        first += out.shape[1]


def phase(*values):
    return lax.optimization_barrier(values)


def flip(a, axis, bit):
    return lax.ppermute(a, axis, [(i, i ^ bit) for i in range(lax.axis_size(axis))])


def add_body(*refs):
    *sources, out = refs
    out[...] = sum(ref[...].astype(F32) for ref in sources).astype(out.dtype)


def add(*terms, kind=BF16, cost=1):
    spec = pl.BlockSpec(memory_space=pltpu.VMEM)
    return pl.pallas_call(
        add_body,
        out_shape=jax.ShapeDtypeStruct(terms[0].shape, kind),
        in_specs=[spec] * len(terms),
        out_specs=spec,
        compiler_params=pltpu.CompilerParams(vmem_limit_bytes=8 << 20),
        cost_estimate=pl.CostEstimate(flops=cost << 20, bytes_accessed=1 << 14, transcendentals=0),
    )(*terms)


def half_body(first, *refs):
    *sources, out_ref, sum_ref, sem = refs
    sources = sources[-3:]
    sum_ref[...] = sum(ref[...].astype(F32) for ref in sources)
    columns = out_ref.at[:, pl.ds(first, sum_ref.shape[1])]
    copy = pltpu.make_async_copy(sum_ref, columns, sem)
    copy.start()
    copy.wait()


def half_sum(first, width, out, *terms, cost=1):
    rows, part = terms[0].shape
    spec = pl.BlockSpec(memory_space=pltpu.VMEM)
    whole = pl.BlockSpec(memory_space=pl.ANY)
    operands = terms if out is None else (out, *terms)
    return pl.pallas_call(
        functools.partial(half_body, first),
        out_shape=jax.ShapeDtypeStruct((rows, width), F32),
        in_specs=([] if out is None else [whole]) + [spec] * len(terms),
        out_specs=whole,
        scratch_shapes=[pltpu.VMEM((rows, part), F32), pltpu.SemaphoreType.DMA],
        input_output_aliases={} if out is None else {0: 0},
        compiler_params=pltpu.CompilerParams(vmem_limit_bytes=8 << 20),
        cost_estimate=pl.CostEstimate(flops=cost << 20, bytes_accessed=1 << 14, transcendentals=0),
    )(*operands)


def small(body, kind, *terms, wide=1):
    spec = pl.BlockSpec(memory_space=pltpu.VMEM)
    return pl.pallas_call(
        body,
        out_shape=jax.ShapeDtypeStruct((terms[0].shape[0], terms[0].shape[1] * wide), kind),
        in_specs=[spec] * len(terms),
        out_specs=spec,
        compiler_params=pltpu.CompilerParams(vmem_limit_bytes=8 << 20),
        cost_estimate=pl.CostEstimate(flops=1 << 20, bytes_accessed=1 << 14, transcendentals=0),
    )(*terms)


class Scan:
    def __init__(self, term, later):
        self.term, self.later, self.total, self.before = term, later, term, 0.0
        self.bits = [1 << i for i in range(lax.axis_size("seq").bit_length() - 1)]

    def inside(self, bit):
        return ((lax.axis_index("seq") & bit) != 0) != self.later

    def start(self, bit):
        return flip(self.total, "seq", bit)

    def take(self, bit, got):
        self.before += jnp.where(self.inside(bit), got, 0).astype(F32)
        self.total = add(self.total, got)

    def across(self):
        own = jnp.where(self.inside(1), 0, self.term).astype(F32)
        return flip((self.before + own).astype(BF16), "seq", 1)

    def result(self, got=0.0):
        return (self.before + got).astype(BF16)


def send(a, pairs):
    return lax.ppermute(a, "seq", [(2 * s + i, 2 * t + i) for s, t in pairs for i in range(2)])


OUTER = ((0, 1), (1, 0), (2, 3), (3, 2))
MIDDLE = ((1, 2), (2, 1))
ORDER = ((3, 2, 1, 0), (3, 2, 0, 1), (0, 1, 3, 2), (0, 1, 2, 3))


def per_device(queries, keys, values, out_grad, out_weight):
    rows, width = queries.shape
    n_seq, n_head = lax.axis_size("seq"), lax.axis_size("head")
    seq = lax.axis_index("seq")
    y = seq % 2
    line = n_seq // 2
    total = n_seq * rows
    scale = 1.0 / math.sqrt(HD * total)
    factor = 1.0 / math.sqrt(total)
    part = 256
    shaped = lambda dims, dtype=BF16: jax.ShapeDtypeStruct(dims, dtype)
    state = functools.partial(state_body, scale)
    state_shape = shaped((width, HD))

    cols = out_grad.shape[1]
    block = cols * n_head // n_seq
    short = line == 4 and n_head == 4

    def half(a, i):
        cut = a.reshape(rows, cols // (2 * block), 2, block)
        return lax.dynamic_index_in_dim(cut, i, 2, keepdims=False).reshape(rows, cols // 2)

    inner = functools.partial(inner_body, scale, part)
    outputs = outputs_body
    matrix = shaped((rows, width))

    def product(slots, kinds, *operands, cost=1):
        body = functools.partial(product_body, factor, n_head, short, slots, [len(k) for k in kinds])
        outs = [shaped((cols // 2, width // len(k)), kind) for k in kinds for kind in k]
        like = [((rows, cols // 2), BF16)] * (2 * len(slots))
        scratch = [((rows, width), BF16)] * 2 + like
        return call(body, outs, *operands, scratch=scratch, cost=cost, vmem=60)

    by_x = flip(out_grad, "head", 2)
    if short:
        scratch = [((rows, width), BF16)] * 2
        outs = [state_shape, shaped((rows, cols // 2))]
        kv_term, other = call(state, outs, keys, values, out_grad, scratch=scratch, vmem=60)
    else:
        (kv_term,), other = call(state, [state_shape], keys, values), half(out_grad, 1 - y)
    prior = Scan(kv_term, False)
    got = prior.start(1)
    got, other, q, grad = phase(got, other, queries, out_grad)
    near = flip(other, "seq", 1)
    by_core = flip(grad, "head", 1)
    prior.take(1, got)
    for bit in prior.bits[1:]:
        got = prior.start(bit)
        if bit == 4:
            (pv,) = call(inner, [shaped((rows, width), F32)], q, keys, values)
            got, pv, grad, by_x, near = phase(got, pv, grad, by_x, near)
        prior.take(bit, got)
    prior = prior.result()

    (o,) = call(outputs, [matrix], prior, queries, pv)
    o, by_x, near = phase(o, by_x, near)
    n = flip(o, "seq", 1)
    far = flip(near, "head", 2)
    by_xc = flip(by_x, "head", 1)

    pieces = [out_grad, by_core, by_x, by_xc]
    mine = pieces if short else [half(p, y) for p in pieces]
    (attn_grad,) = call(attn_grad_body, [matrix], out_weight, *pieces)
    (back_term,) = call(state, [state_shape], queries, attn_grad)
    later = Scan(back_term, True)
    got = later.start(2)
    if short:
        first = functools.partial(first_body, factor, n_head)
        scratch = [((rows, cols // 2), BF16), ((rows, width), BF16)]
        outs = [shaped((cols // 2, width), F32)]
        o, near, back_term = phase(o, near, back_term)
        near_c = flip(near, "head", 1)
        (begun,) = call(functools.partial(first, True), outs, o, *mine, scratch=scratch, vmem=12)
        got, n, far, begun = phase(got, n, far, begun)
    else:
        near_c = flip(near, "head", 1)
        got, n, far = phase(got, n, far)
    far_c = flip(far, "head", 1)
    later.take(2, got)
    operands = (o, n, *mine, near, near_c, far, far_c)

    def gradients(later):
        body = functools.partial(grads_body, scale, part)
        return call(body, [matrix] * 3, queries, keys, values, attn_grad, prior, later)

    if short:
        got = later.start(4)
        pair = (BF16, BF16)
        outs = [shaped((cols // 2, width // 2))] * 2
        theirs = (near, near_c, far, far_c)
        first = functools.partial(first, False)
        b0 = call(first, outs, n, *theirs, begun, scratch=scratch[:1], vmem=8, direct=(0, n_head + 1))
        e1 = [send(b, OUTER) for b in b0]
        o, got, *b0 = phase(o, got, *b0)
        outs = product((1, 2, 3), (pair, (F32, F32), (F32, F32)), o, *operands[1:], cost=1 << 14)
        b1, b2, (b3, b3_back) = list(outs[:2]), outs[2:4], outs[4:]
        e2 = [send(b1[0], OUTER)]
        later.take(4, got)
        got = later.across()
        e1[0], b1[1], got, *b2 = phase(e1[0], b1[1], got, *b2)
        m2 = [send(add(b0[0], e1[0]), MIDDLE)]
        e2 += [send(b1[1], OUTER)]
        m2 += [send(add(b0[1], e1[1], cost=1024), MIDDLE)]
        e2[0], m2[0] = phase(e2[0], m2[0])
        sent = add(b1[0], e2[0], cost=2048)
        m3 = [send(sent, MIDDLE)]
        m2[1], got, _ = phase(m2[1], got, sent)
        parts = [add(b, m) for b, m in zip(b2, m2)]
        e3 = [send(p, OUTER) for p in parts]
        e2[1], _, _ = phase(e2[1], *parts)
        m3 += [send(add(b1[1], e2[1]), MIDDLE)]
        grads = gradients(later.result(got))
        weight_grad = half_sum(0, width, None, b3, m3[0], e3[0], cost=2048)
        weight_grad = half_sum(width // 2, width, weight_grad, b3_back, m3[1], e3[1])
    else:
        for bit in later.bits[1:]:
            later.take(bit, later.start(bit))
        grads = gradients(later.result(later.across()))
        groups = [[2 * p + i for p in range(line)] for i in range(2)]
        whole = jnp.concatenate(product(range(n_head), [(F32,)] * n_head, *operands), axis=0)
        weight_grad = lax.psum_scatter(
            whole, "seq", scatter_dimension=0, axis_index_groups=groups, tiled=True
        )
    return (*grads, weight_grad)


def solution(mesh):
    return jax.shard_map(
        per_device,
        mesh=mesh,
        in_specs=(
            P("seq", "head"),
            P("seq", "head"),
            P("seq", "head"),
            P("seq", "head"),
            P(None, "head"),
        ),
        out_specs=(P("seq", "head"), P("seq", "head"), P("seq", "head"), P("seq", "head")),
        check_vma=False,
    )
```
